512 devices in a mesh: tile: 64 (over z_hi, y, core), vert: 2 (over z_lo), dir: 4 (over x).
Axes of the slice: x: 4, y: 8, z: 8 (z_hi: 4, z_lo: 2; z = z_hi * 2 + z_lo), core: 2. Of those that a mesh axis runs over, the one named last changes fastest.
Arguments:
- tangent_in: float32 [8, 3, 64, 256, 128], P('dir', None, 'vert', 'tile'), may hold values from -6 to 6
- records: bfloat16 [16, 4, 64, 256, 128], P('dir', None, 'vert', 'tile'), may hold values from -2 to 10, as said below
- record_slot: int32 [16], replicated, may hold values from 0 to 15, each once
- step_record: int32 [2], replicated, may hold values from 0 to 15
- turbine_mask: int32 [64, 256, 128], P('vert', 'tile'), may hold values from 0 to 8
- group_weights: float32 [8, 8], P('dir'), may hold values from -1.2 to 1.2
Outputs:
- tangent_out: float32 [8, 3, 64, 256, 128], P('dir', None, 'vert', 'tile')
- power: float32 [8], P('dir')
The draws below stay inside these ranges and needn't reach their ends.
Inputs may be any that keep to these rules, and one draw needn't show every extreme that they name: `records`: component 0 of every record lies in [4, 10], component 1 in [-2, 2], component 2 in [-1, 1], component 3 in [0.05, 0.5]. `record_slot`: each record is stored in exactly one slot.
All inputs are finite; a program needn't handle non-finite values.
Results may differ from the reference program's by a relative error of at most 0.0003.
Values may be sent and summed in bfloat16 or wider, within the bound.
No kernel may reach another device: no remote copies, remote signals or barrier semaphores. Data moves between devices by JAX's collectives and lax.ppermute only.
A program may use at most 64 MiB of HBM per device.

```python
import math
import jax
import jax.numpy as jnp
from jax import lax

NY = 128
NZ = 64
GROUPS = 8
STEPS = 2
NDIR = 8
NREC = 16
NX = 256


def draw_records(key, part):
    keys = jax.random.split(key, 4)
    shape = (NREC, NZ, NX, NY)
    streamwise = jnp.clip(7.0 + 1.5 * jax.random.normal(keys[0], shape, jnp.float32), 4.0, 10.0)
    spanwise = jax.random.uniform(keys[1], shape, jnp.float32, -2.0, 2.0)
    upward = jax.random.uniform(keys[2], shape, jnp.float32, -1.0, 1.0)
    viscosity = jnp.exp(jax.random.uniform(keys[3], shape, jnp.float32, math.log(0.05), math.log(0.5)))
    return jnp.stack([streamwise, spanwise, upward, viscosity], axis=1).astype(jnp.bfloat16)


def place_ends(drawn, stream_key, smallest, largest):
    shape = drawn.shape
    spot = [jax.random.randint(jax.random.fold_in(stream_key, axis), (), 0, shape[axis]) for axis in range(len(shape))]
    drawn = drawn.at[tuple(spot)].set(smallest)
    longest = shape.index(max(shape))
    spot[longest] = (spot[longest] + 1) % shape[longest]
    return drawn.at[tuple(spot)].set(largest)


def block_scale(key, extent, cuts, smallest, high):
    gain, own = 1.0, jax.random.fold_in(key, 6)
    for dim, blocks in cuts:
        heights = jnp.exp(jax.random.uniform(jax.random.fold_in(own, dim), (blocks,), jnp.float32, smallest / len(cuts), high / len(cuts)))
        gain = gain * jnp.repeat(heights, extent[dim] // blocks).reshape([-1 if axis == dim else 1 for axis in range(len(extent))])
    return gain


def bell_draw(key, dims, scale, bound, pieces=(), held_as=jnp.bfloat16):
    entries = scale * jax.random.normal(key, dims, jnp.float32)
    if pieces:
        entries = entries * block_scale(key, dims, pieces, -0.22, 0.18)
    return jnp.clip(entries, -bound, bound).astype(held_as)


def setup_inputs(seed: int = 0) -> dict:
    splits = jax.random.split(jax.random.key(seed), 7)
    return {
        "tangent_in": bell_draw(splits[0], (NDIR, 3, NZ, NX, NY), 1.0, 6.0, ((0, 4), (2, 2), (3, 64)), jnp.float32),
        "records": draw_records(jax.random.fold_in(splits[6], 71), 0),
        "record_slot": jax.random.permutation(splits[2], NREC).astype(jnp.int32),
        "step_record": jax.random.randint(splits[3], (STEPS,), 0, NREC).astype(jnp.int32),
        "turbine_mask": place_ends(jax.random.randint(splits[4], (NZ, NX, NY), 0, GROUPS + 1), jax.random.fold_in(splits[4], 1), 0, GROUPS).astype(jnp.int32),
        "group_weights": bell_draw(splits[5], (NDIR, GROUPS), 0.2, 1.2, ((0, 4),), jnp.float32),
    }


TIME_STEP = 0.05
DRAG_COEFF = 0.5
POWER_SCALE = 0.01
VERTICAL_ASPECT = 400.0

def shifted(padded, offset):
    inner_count = padded.shape[-2] - 4
    return lax.slice_in_dim(padded, 2 + offset, 2 + offset + inner_count, axis=padded.ndim - 2)

def x_slope(padded):
    return (8.0 * (shifted(padded, 1) - shifted(padded, -1)) - (shifted(padded, 2) - shifted(padded, -2))) / 12.0

def x_curve(padded):
    return shifted(padded, 1) - 2.0 * shifted(padded, 0) + shifted(padded, -1)

def y_slope(values_in):
    return (8.0 * (jnp.roll(values_in, -1, axis=-1) - jnp.roll(values_in, 1, axis=-1)) - (jnp.roll(values_in, -2, axis=-1) - jnp.roll(values_in, 2, axis=-1))) / 12.0

def y_curve(values_in):
    return jnp.roll(values_in, -1, axis=-1) - 2.0 * values_in + jnp.roll(values_in, 1, axis=-1)

def z_slope(values_in):
    axis_z = values_in.ndim - 3
    widths = [(0, 0)] * values_in.ndim
    widths[axis_z] = (1, 1)
    padded = jnp.pad(values_in, widths)
    levels = values_in.shape[axis_z]
    return 0.5 * (lax.slice_in_dim(padded, 2, 2 + levels, axis=axis_z) - lax.slice_in_dim(padded, 0, levels, axis=axis_z))

def pad_streamwise(values_in):
    return jnp.pad(values_in, [(0, 0)] * (values_in.ndim - 2) + [(2, 2), (0, 0)])

def turbine_terms(turbine_mask, group_weights):
    turbine = (turbine_mask > 0).astype(jnp.float32)
    source = jnp.zeros((group_weights.shape[0],) + turbine_mask.shape, jnp.float32)
    for group_id in range(group_weights.shape[1]):
        source = source + (turbine_mask == group_id + 1).astype(jnp.float32)[None] * group_weights[:, group_id][:, None, None, None]
    return (turbine, source)

def horizontal_update(tangent, tangent_pad, background, background_pad, turbine, source):
    velocity = background[:3]
    viscosity = background[3]
    wind_speed = jnp.sqrt(velocity[0] * velocity[0] + velocity[1] * velocity[1])
    advect = velocity[0] * x_slope(tangent_pad) + velocity[1] * y_slope(tangent)
    produce = tangent[:, 0:1] * x_slope(background_pad)[None] + tangent[:, 1:2] * y_slope(velocity)[None]
    spread = viscosity * (x_curve(tangent_pad) + y_curve(tangent))
    parallel = (velocity[0] * tangent[:, 0] + velocity[1] * tangent[:, 1]) / wind_speed
    drag_term = -DRAG_COEFF * turbine * (wind_speed * tangent + velocity[None] * parallel[:, None])
    forcing = -source[:, None] * (wind_speed * velocity)[None]
    return tangent + TIME_STEP * (spread + drag_term + forcing - advect - produce)

def column_solve(rhs_levels, viscosity):
    stiff = VERTICAL_ASPECT * viscosity
    interior = 0.5 * (stiff[:-1] + stiff[1:])
    face_lower = jnp.concatenate([stiff[:1], interior], axis=0)
    face_upper = jnp.concatenate([interior, stiff[-1:]], axis=0)
    coeff_below = -TIME_STEP * face_lower
    coeff_above = -TIME_STEP * face_upper
    diagonal_main = 1.0 + TIME_STEP * (face_lower + face_upper)
    levels = jnp.moveaxis(rhs_levels, -3, 0)

    def forward(carried, inputs):
        ratio_prev, value_prev = carried
        below_now, center_now, above_now, rhs_now = inputs
        pivot_value = center_now - below_now * ratio_prev
        ratio_now = above_now / pivot_value
        value_now = (rhs_now - below_now * value_prev) / pivot_value
        return ((ratio_now, value_now), (ratio_now, value_now))
    initial = (jnp.zeros(viscosity.shape[1:], jnp.float32), jnp.zeros(levels.shape[1:], jnp.float32))
    _, (ratios, values) = lax.scan(forward, initial, (coeff_below, diagonal_main, coeff_above, levels))

    def backward(next_value, inputs):
        ratio_now, value_now = inputs
        result = value_now - ratio_now * next_value
        return (result, result)
    _, solved = lax.scan(backward, jnp.zeros(levels.shape[1:], jnp.float32), (ratios, values), reverse=True)
    return jnp.moveaxis(solved, 0, -3)

def vertical_update(tangent, partial_value, background):
    velocity = background[:3]
    vertical_terms = background[2] * z_slope(tangent) + tangent[:, 2:3] * z_slope(velocity)[None]
    return column_solve(partial_value - TIME_STEP * vertical_terms, background[3])

def power_terms(tangent, background, turbine):
    velocity = background[:3]
    wind_speed = jnp.sqrt(velocity[0] * velocity[0] + velocity[1] * velocity[1])
    return lax.optimization_barrier(jnp.sum(turbine * wind_speed * (velocity[0] * tangent[:, 0] + velocity[1] * tangent[:, 1]), axis=(1, 2, 3)))

def reference(tangent_in, records, record_slot, step_record, turbine_mask, group_weights):
    turbine, source = turbine_terms(turbine_mask, group_weights)
    finals = []
    sums = []
    for direction in range(NDIR):
        tangent = tangent_in[direction:direction + 1]
        power_sum = jnp.zeros((1,), jnp.float32)
        for step_no in range(STEPS):
            slot_index = record_slot[step_record[step_no]]
            background = lax.dynamic_index_in_dim(records, slot_index, 0, keepdims=False).astype(jnp.float32)
            partial_value = horizontal_update(tangent, pad_streamwise(tangent), background, pad_streamwise(background[:3]), turbine, source[direction:direction + 1])
            tangent = vertical_update(tangent, partial_value, background)
            power_sum = power_sum + power_terms(tangent, background, turbine)
        finals.append(tangent)
        sums.append(power_sum)
    power_factor = POWER_SCALE / math.sqrt(NX * NY * NZ)
    return (jnp.concatenate(finals, axis=0), jnp.concatenate(sums, axis=0) * power_factor)
```

```python
import functools
import math

import jax
import jax.numpy as jnp
from jax import lax
from jax.experimental import pallas as pl
from jax.experimental.pallas import tpu as pltpu
from jax.sharding import Mesh
from jax.sharding import PartitionSpec as P

STEPS = 2
TIME_STEP = 0.05
DRAG_COEFF = 0.5
POWER_SCALE = 0.01
VERTICAL_ASPECT = 400.0
TILE = ("row", "core")
HALF = 0.5 * TIME_STEP
FACE = 0.5 * TIME_STEP * VERTICAL_ASPECT

RHS, DIAG, VISC, WIND, RAW, DIAG2, VISC2, WIND2, WROW, FIELDS = 0, 6, 7, 8, 11, 17, 18, 19, 22, 24


def window(ref, field, level, offset=0):
    return ref[field, level, 2 + offset : 10 + offset, :]


def roll_y(values, offset):
    return pltpu.roll(values, (-offset) % values.shape[-1], 1)


def wind_terms(winds, turbines, level, above, below, sign, beyond=None):
    wind = [window(winds, c, level) for c in range(3)]
    visc = TIME_STEP * window(winds, 3, level)
    mask = turbines[level, 2:10, :]
    turbine = jnp.where(mask > 0.5, 1.0, 0.0)
    square = wind[0] * wind[0] + wind[1] * wind[1]
    inverse = lax.rsqrt(square)
    speed = square * inverse
    drag = (DRAG_COEFF * TIME_STEP) * turbine
    along = drag * inverse
    by_first, by_second, by_third = [], [], []
    for c in range(3):
        near = window(winds, c, level, 1) - window(winds, c, level, -1)
        far = window(winds, c, level, 2) - window(winds, c, level, -2)
        slope = (TIME_STEP * 8.0 / 12.0) * near - (TIME_STEP / 12.0) * far
        by_first.append(slope + along * wind[c] * wind[0])
        near = roll_y(wind[c], 1) - roll_y(wind[c], -1)
        far = roll_y(wind[c], 2) - roll_y(wind[c], -2)
        slope = (TIME_STEP * 8.0 / 12.0) * near - (TIME_STEP / 12.0) * far
        by_second.append(slope + along * wind[c] * wind[1])
        vertical = jnp.zeros_like(speed)
        if beyond is not None:
            vertical = vertical + beyond[c]
        elif above is not None:
            vertical = vertical + window(winds, c, above)
        if below is not None:
            vertical = vertical - window(winds, c, below)
        by_third.append((HALF * sign) * vertical)
    first = (TIME_STEP * 8.0 / 12.0) * wind[0]
    second = (TIME_STEP * 8.0 / 12.0) * wind[1]
    return dict(
        wind=wind,
        mask=mask,
        turbine=turbine,
        speed=speed,
        center=1.0 - 4.0 * visc - drag * speed,
        x_up=visc - first,
        x_down=visc + first,
        x_far=0.125 * first,
        y_up=visc - second,
        y_down=visc + second,
        y_far=0.125 * second,
        z=(HALF * sign) * wind[2],
        by=(by_first, by_second, by_third),
    )


def right_side(tangents, weights, terms, level, above, below, beyond=None):
    speed_step = TIME_STEP * terms["speed"]
    groups = weights.shape[1]
    hits = [terms["mask"] == float(g + 1) for g in range(groups)]
    rows = []
    for d in range(weights.shape[0]):
        source = jnp.zeros_like(speed_step)
        for g in range(groups):
            source = jnp.where(hits[g], weights[d, g], source)
        force = source * speed_step
        own = [window(tangents, 3 * d + i, level) for i in range(3)]
        for i in range(3):
            field = 3 * d + i
            value = terms["center"] * own[i]
            value += terms["x_up"] * window(tangents, field, level, 1)
            value += terms["x_down"] * window(tangents, field, level, -1)
            value += terms["x_far"] * (
                window(tangents, field, level, 2) - window(tangents, field, level, -2)
            )
            value += terms["y_up"] * roll_y(own[i], 1)
            value += terms["y_down"] * roll_y(own[i], -1)
            value += terms["y_far"] * (roll_y(own[i], 2) - roll_y(own[i], -2))
            vertical = None
            if beyond is not None:
                vertical = beyond[field]
            elif above is not None:
                vertical = window(tangents, field, above)
            if below is not None:
                lower = window(tangents, field, below)
                vertical = -lower if vertical is None else vertical - lower
            if vertical is not None:
                value -= terms["z"] * vertical
            for c in range(3):
                value -= terms["by"][c][i] * own[c]
            value -= force * terms["wind"][i]
            rows.append(value)
    return rows


def first_kernel(place, weights, left, own, right, low, high, rec_a, rec_b, groups,
                 message, ratio_out, value_out, power_out, ratio2_out, inverse2_out, face2_out,
                 wrow_out, tangents, winds, winds2, turbines):
    levels = own.shape[2]
    last = levels - 1
    sign = place[0].astype(jnp.float32)
    base = place[1]
    step = place[0]

    def at(j):
        return base + step * j

    for field in range(6):
        d, i = divmod(field, 3)
        tangents[field, :, 0:4, :] = left[d, i]
        tangents[field, :, 4:8, :] = own[d, i]
        tangents[field, :, 8:12, :] = right[d, i]
    for c in range(4):
        winds[c, :, 0:4, :] = low[c].astype(jnp.float32)
        winds[c, :, 4:8, :] = rec_a[c].astype(jnp.float32)
        winds[c, :, 8:12, :] = high[c].astype(jnp.float32)
        winds2[c, :, 4:8, :] = rec_b[c].astype(jnp.float32)
    turbines[:, 0:4, :] = low[7].astype(jnp.float32)
    turbines[:, 4:8, :] = groups[...].astype(jnp.float32)
    turbines[:, 8:12, :] = high[7].astype(jnp.float32)

    def level_rows(j, above, below):
        k = at(j)
        terms = wind_terms(winds, turbines, k, above, below, sign)
        rows = right_side(tangents, weights, terms, k, above, below)
        for c in range(2):
            power_out[c, k] = terms["turbine"] * terms["speed"] * terms["wind"][c]
        wind2 = [window(winds2, c, k) for c in range(2)]
        square = wind2[0] * wind2[0] + wind2[1] * wind2[1]
        scale = terms["turbine"] * (square * lax.rsqrt(square))
        return rows, [scale * wind2[0], scale * wind2[1]]

    def eliminate(j, above, below, carry):
        face_prev, ratio_prev, values_prev, face2_prev, ratio2_prev, w_prev = carry
        k = at(j)
        rows, wrows = level_rows(j, above, below)
        face = FACE * (window(winds, 3, k) + window(winds, 3, above))
        inverse = 1.0 / (1.0 + face + face_prev * (1.0 - ratio_prev))
        ratio = face * inverse
        values = [(r + face_prev * v) * inverse for r, v in zip(rows, values_prev)]
        ratio_out[k] = ratio
        for field in range(6):
            value_out[field, k] = values[field]
        face2 = FACE * (window(winds2, 3, k) + window(winds2, 3, above))
        inverse2 = 1.0 / (1.0 + face2 + face2_prev * (1.0 - ratio2_prev))
        ratio2 = face2 * inverse2
        ws = [(r + face2_prev * v) * inverse2 for r, v in zip(wrows, w_prev)]
        ratio2_out[k] = ratio2
        inverse2_out[k] = inverse2
        face2_out[k] = face2
        for c in range(2):
            wrow_out[c, k] = ws[c]
        return face, ratio, tuple(values), face2, ratio2, tuple(ws)

    zero = jnp.zeros((8, own.shape[4]), jnp.float32)
    carry = (
        (2.0 * FACE) * window(winds, 3, at(0)), zero, (zero,) * 6,
        (2.0 * FACE) * window(winds2, 3, at(0)), zero, (zero,) * 2,
    )
    carry = eliminate(0, at(1), None, carry)
    carry = lax.fori_loop(
        1, last, lambda j, c: eliminate(j, at(j + 1), at(j - 1), c), carry
    )
    face, ratio, values, face2, ratio2, ws = carry
    k = at(last)
    rows, wrows = level_rows(last, None, at(last - 1))
    for field in range(6):
        message[RHS + field] = rows[field] + face * values[field]
        message[RAW + field] = window(tangents, field, k)
    message[DIAG] = 1.0 + face * (1.0 - ratio)
    message[VISC] = window(winds, 3, k)
    message[DIAG2] = 1.0 + face2 * (1.0 - ratio2)
    message[VISC2] = window(winds2, 3, k)
    for c in range(3):
        message[WIND + c] = window(winds, c, k)
        message[WIND2 + c] = window(winds2, c, k)
    for c in range(2):
        message[WROW + c] = wrows[c] + face2 * ws[c]


def second_kernel(place, weights, mine, theirs, ratio_in, value_in, power_in, ratio2_in, inverse2_in,
                  face2_in, wrow_in, low, high, rec_b, groups,
                  row_out, value_out, middle_out, sums_out, tangents, winds, turbines, adjoint):
    levels = rec_b.shape[1]
    last = levels - 1
    sign = place[0].astype(jnp.float32)
    base = place[1]
    step = place[0]

    def at(j):
        return base + step * j

    for c in range(3):
        winds[c, :, 0:4, :] = low[4 + c].astype(jnp.float32)
        winds[c, :, 8:12, :] = high[4 + c].astype(jnp.float32)
    for c in range(4):
        winds[c, :, 4:8, :] = rec_b[c].astype(jnp.float32)
    turbines[:, 4:8, :] = groups[...].astype(jnp.float32)

    zero = jnp.zeros((8, rec_b.shape[3]), jnp.float32)
    layer = lax.broadcasted_iota(jnp.int32, zero.shape, 0)
    inside = jnp.logical_and(layer >= place[2], layer < place[3])
    center = jnp.logical_and(layer >= 2, layer < 6)

    face = FACE * (mine[VISC] + theirs[VISC])
    pivot, pivot_far = mine[DIAG] + face, theirs[DIAG] + face
    inverse = 1.0 / (pivot * pivot_far - face * face)
    nexts, beyond = [], []
    for field in range(6):
        d, i = divmod(field, 3)
        row = mine[RHS + field] - (HALF * sign) * (
            mine[WIND + 2] * theirs[RAW + field] + mine[RAW + 3 * d + 2] * theirs[WIND + i]
        )
        row_far = theirs[RHS + field] + (HALF * sign) * (
            theirs[WIND + 2] * mine[RAW + field] + theirs[RAW + 3 * d + 2] * mine[WIND + i]
        )
        nexts.append(jnp.where(inside, (row * pivot_far + face * row_far) * inverse, 0.0))
        beyond.append(jnp.where(inside, (row_far * pivot + face * row) * inverse, 0.0))
    face2 = FACE * (mine[VISC2] + theirs[VISC2])
    pivot, pivot_far = mine[DIAG2] + face2, theirs[DIAG2] + face2
    inverse = 1.0 / (pivot * pivot_far - face2 * face2)
    near_part, far_part = pivot_far * inverse, face2 * inverse
    middle_out[0] = near_part
    middle_out[1] = far_part
    ws = [near_part * mine[WROW + c] + far_part * theirs[WROW + c] for c in range(2)]

    def keep(k, values, ws, sums):
        for field in range(6):
            tangents[field, k, 2:10, :] = values[field]
        for c in range(2):
            adjoint[c, k] = ws[c]
        return tuple(
            sums[d] + power_in[0, k] * values[3 * d] + power_in[1, k] * values[3 * d + 1]
            for d in range(2)
        )

    sums = keep(at(last), nexts, ws, (zero, zero))

    def back(n, carry):
        values, ws, sums = carry
        k = at(last - 1 - n)
        ratio = ratio_in[k]
        values = tuple(
            jnp.where(inside, value_in[f, k] + ratio * values[f], 0.0) for f in range(6)
        )
        ratio2 = ratio2_in[k]
        ws = tuple(wrow_in[c, k] + ratio2 * ws[c] for c in range(2))
        return values, ws, keep(k, values, ws, sums)

    _, _, sums = lax.fori_loop(0, last, back, (tuple(nexts), tuple(ws), sums))

    def level_rows(j, above, below, sums, winds_beyond=None, values_beyond=None):
        k = at(j)
        terms = wind_terms(winds, turbines, k, above, below, sign, winds_beyond)
        rows = right_side(tangents, weights, terms, k, above, below, values_beyond)
        sums = tuple(
            sums[d] + adjoint[0, k] * rows[3 * d] + adjoint[1, k] * rows[3 * d + 1]
            for d in range(2)
        )
        return rows, sums

    def eliminate(j, above, below, carry):
        face_prev, values_prev, sums = carry
        k = at(j)
        rows, sums = level_rows(j, above, below, sums)
        inverse = inverse2_in[k]
        values = tuple((r + face_prev * v) * inverse for r, v in zip(rows, values_prev))
        for field in range(6):
            value_out[field, k] = values[field]
        return face2_in[k], values, sums

    carry = eliminate(0, at(1), None, (zero, (zero,) * 6, sums))
    face, values, sums = lax.fori_loop(
        1, last, lambda j, c: eliminate(j, at(j + 1), at(j - 1), c), carry
    )
    rows, sums = level_rows(
        last, None, at(last - 1), sums, [theirs[WIND2 + c] for c in range(3)], beyond
    )
    for field in range(6):
        row_out[field] = rows[field] + face * values[field]
    for d in range(2):
        sums_out[d : d + 1, :] = jnp.sum(jnp.where(center, sums[d], 0.0), axis=0, keepdims=True)


def third_kernel(place, mine, theirs, middle, ratio_in, value_in, out):
    levels = ratio_in.shape[0]
    last = levels - 1
    base = place[1]
    step = place[0]
    values = tuple(middle[0] * mine[f] + middle[1] * theirs[f] for f in range(6))

    def keep(k, values):
        for field in range(6):
            d, i = divmod(field, 3)
            out[d, i, k] = values[field][2:6]

    keep(base + step * last, values)

    def back(n, values):
        k = base + step * (last - 1 - n)
        ratio = ratio_in[k]
        values = tuple(value_in[f, k] + ratio * values[f] for f in range(6))
        keep(k, values)
        return values

    lax.fori_loop(0, last, back, values)


def call(kernel, scalars, arrays, outs, scratch):
    return pl.pallas_call(
        kernel,
        out_shape=[jax.ShapeDtypeStruct(shape, jnp.float32) for shape in outs],
        in_specs=[pl.BlockSpec(memory_space=pltpu.SMEM)] * len(scalars)
        + [pl.BlockSpec(memory_space=pltpu.VMEM)] * len(arrays),
        out_specs=[pl.BlockSpec(memory_space=pltpu.VMEM)] * len(outs),
        scratch_shapes=[pltpu.VMEM(shape, jnp.float32) for shape in scratch],
        compiler_params=pltpu.CompilerParams(vmem_limit_bytes=40 * 1024 * 1024),
    )(*scalars, *arrays)


def fetch_records(first, second, owner_first, owner_second):
    count = lax.axis_size("dir")
    here = lax.axis_index("dir")

    def spread(record, owner):
        result = record
        for k in range(1, count):
            target = (owner + k) % count
            got = lax.ppermute(record, "dir", [(owner, target)])
            result = jnp.where(here == target, got, result)
        return result

    def branch(a, b):
        return lambda x, y: (spread(x, a), spread(y, b))

    branches = [branch(a, b) for a in range(count) for b in range(count)]
    return lax.switch(owner_first * count + owner_second, branches, first, second)


def shards(tangent_in, records, record_slot, step_record, turbine_mask, group_weights):
    directions, components, levels, layers, spans = tangent_in.shape
    fields = directions * components
    tiles = lax.axis_size("row") * lax.axis_size("core")
    tile = lax.axis_index("row") * lax.axis_size("core") + lax.axis_index("core")
    vert = lax.axis_index("vert")
    up = [(i, i + 1) for i in range(tiles - 1)]
    down = [(i + 1, i) for i in range(tiles - 1)]
    swap = [(0, 1), (1, 0)]
    per_device = records.shape[0]

    left = lax.ppermute(tangent_in, TILE, up)
    right = lax.ppermute(tangent_in, TILE, down)

    slots = [record_slot[step_record[s]] for s in range(STEPS)]
    stored = [lax.dynamic_index_in_dim(records, s % per_device, 0, keepdims=False) for s in slots]
    rec_a, rec_b = fetch_records(*stored, *[s // per_device for s in slots])

    edge = jnp.concatenate([rec_a, rec_b[:3], turbine_mask.astype(jnp.bfloat16)[None]], axis=0)
    low = lax.ppermute(edge, TILE, up)
    high = lax.ppermute(edge, TILE, down)

    place = jnp.stack([
        1 - 2 * vert,
        vert * (levels - 1),
        jnp.where(tile == 0, 2, 0),
        jnp.where(tile == tiles - 1, 6, 8),
    ]).astype(jnp.int32)

    def block(*lead):
        return (*lead, 8, spans)

    def wide(*lead):
        return (*lead, 16, spans)

    message, ratio, value, power, ratio2, inverse2, face2, wrow = call(
        first_kernel,
        (place, group_weights),
        (left, tangent_in, right, low, high, rec_a, rec_b, turbine_mask),
        (block(FIELDS), block(levels), block(fields, levels), block(2, levels),
         block(levels), block(levels), block(levels), block(2, levels)),
        (wide(fields, levels), wide(4, levels), wide(4, levels), wide(levels)),
    )
    answer = lax.ppermute(message, "vert", swap)
    row, value2, middle, sums = call(
        second_kernel,
        (place, group_weights),
        (message, answer, ratio, value, power, ratio2, inverse2, face2, wrow, low, high, rec_b, turbine_mask),
        (block(fields), block(fields, levels), block(2), (directions, spans)),
        (wide(fields, levels), wide(4, levels), wide(levels), block(2, levels)),
    )
    answer2 = lax.ppermute(row, "vert", swap)

    sums = lax.psum(sums, "core")
    count = lax.axis_size("row") * lax.axis_size("vert")
    gathered = lax.all_to_all(
        jnp.broadcast_to(sums[None], (count, directions, spans)), ("row", "vert"), 0, 0, tiled=True
    )
    cells = levels * lax.axis_size("vert") * layers * tiles * spans
    power_out = jnp.sum(gathered, axis=(0, 2)) * (POWER_SCALE / math.sqrt(cells))

    (tangent_out,) = call(
        third_kernel,
        (place,),
        (row, answer2, middle, ratio2, value2),
        (tangent_in.shape,),
        (),
    )
    return tangent_out, power_out


def solution(mesh):
    tiles, verts, dirs = mesh.devices.shape
    fine = Mesh(mesh.devices.reshape(tiles // 2, 2, verts, dirs), (*TILE, "vert", "dir"))
    in_specs = (
        P("dir", None, "vert", TILE, None),
        P("dir", None, "vert", TILE, None),
        P(),
        P(),
        P("vert", TILE, None),
        P("dir", None),
    )
    out_specs = (P("dir", None, "vert", TILE, None), P("dir"))
    return jax.shard_map(shards, mesh=fine, in_specs=in_specs, out_specs=out_specs, check_vma=False)
```

```python
import functools
import math

import jax
import jax.numpy as jnp
from jax import lax
from jax.experimental import pallas as pl
from jax.experimental.pallas import tpu as pltpu
from jax.sharding import Mesh
from jax.sharding import PartitionSpec as P

STEPS = 2
TIME_STEP = 0.05
DRAG_COEFF = 0.5
POWER_SCALE = 0.01
VERTICAL_ASPECT = 400.0
TILE = ("row", "core")
HALF = 0.5 * TIME_STEP
FACE = 0.5 * TIME_STEP * VERTICAL_ASPECT

RHS, DIAG, VISC, WIND, RAW, DIAG2, VISC2, WIND2, WROW, FIELDS = 0, 6, 7, 8, 11, 17, 18, 19, 22, 24


def window(ref, field, level, offset=0):
    return ref[field, level, 2 + offset : 10 + offset, :]


def roll_y(values, offset):
    return pltpu.roll(values, (-offset) % values.shape[-1], 1)


def wind_terms(winds, turbines, level, above, below, sign, beyond=None):
    wind = [window(winds, c, level) for c in range(3)]
    visc = TIME_STEP * window(winds, 3, level)
    mask = turbines[level, 2:10, :]
    turbine = jnp.where(mask > 0.5, 1.0, 0.0)
    square = wind[0] * wind[0] + wind[1] * wind[1]
    inverse = lax.rsqrt(square)
    speed = square * inverse
    drag = (DRAG_COEFF * TIME_STEP) * turbine
    along = drag * inverse
    by_first, by_second, by_third = [], [], []
    for c in range(3):
        near = window(winds, c, level, 1) - window(winds, c, level, -1)
        far = window(winds, c, level, 2) - window(winds, c, level, -2)
        slope = (TIME_STEP * 8.0 / 12.0) * near - (TIME_STEP / 12.0) * far
        by_first.append(slope + along * wind[c] * wind[0])
        near = roll_y(wind[c], 1) - roll_y(wind[c], -1)
        far = roll_y(wind[c], 2) - roll_y(wind[c], -2)
        slope = (TIME_STEP * 8.0 / 12.0) * near - (TIME_STEP / 12.0) * far
        by_second.append(slope + along * wind[c] * wind[1])
        vertical = jnp.zeros_like(speed)
        if beyond is not None:
            vertical = vertical + beyond[c]
        elif above is not None:
            vertical = vertical + window(winds, c, above)
        if below is not None:
            vertical = vertical - window(winds, c, below)
        by_third.append((HALF * sign) * vertical)
    first = (TIME_STEP * 8.0 / 12.0) * wind[0]
    second = (TIME_STEP * 8.0 / 12.0) * wind[1]
    return dict(
        wind=wind,
        mask=mask,
        turbine=turbine,
        speed=speed,
        center=1.0 - 4.0 * visc - drag * speed,
        x_up=visc - first,
        x_down=visc + first,
        x_far=0.125 * first,
        y_up=visc - second,
        y_down=visc + second,
        y_far=0.125 * second,
        z=(HALF * sign) * wind[2],
        by=(by_first, by_second, by_third),
    )


def right_side(tangents, weights, terms, level, above, below, beyond=None):
    speed_step = TIME_STEP * terms["speed"]
    groups = weights.shape[1]
    hits = [terms["mask"] == float(g + 1) for g in range(groups)]
    rows = []
    for d in range(weights.shape[0]):
        source = jnp.zeros_like(speed_step)
        for g in range(groups):
            source = jnp.where(hits[g], weights[d, g], source)
        force = source * speed_step
        own = [window(tangents, 3 * d + i, level) for i in range(3)]
        for i in range(3):
            field = 3 * d + i
            value = terms["center"] * own[i]
            value += terms["x_up"] * window(tangents, field, level, 1)
            value += terms["x_down"] * window(tangents, field, level, -1)
            value += terms["x_far"] * (
                window(tangents, field, level, 2) - window(tangents, field, level, -2)
            )
            value += terms["y_up"] * roll_y(own[i], 1)
            value += terms["y_down"] * roll_y(own[i], -1)
            value += terms["y_far"] * (roll_y(own[i], 2) - roll_y(own[i], -2))
            vertical = None
            if beyond is not None:
                vertical = beyond[field]
            elif above is not None:
                vertical = window(tangents, field, above)
            if below is not None:
                lower = window(tangents, field, below)
                vertical = -lower if vertical is None else vertical - lower
            if vertical is not None:
                value -= terms["z"] * vertical
            for c in range(3):
                value -= terms["by"][c][i] * own[c]
            value -= force * terms["wind"][i]
            rows.append(value)
    return rows


def first_kernel(place, weights, mate, own, other, edge_mate, edge, edge_other,
                 message, ratio_out, value_out, power_out, ratio2_out, inverse2_out, face2_out,
                 wrow_out, tangents, winds, winds2, turbines):
    levels = own.shape[2]
    last = levels - 1
    sign = place[0].astype(jnp.float32)
    base = place[1]
    step = place[0]

    def at(j):
        return base + step * j

    for field in range(6):
        d, i = divmod(field, 3)
        tangents[field, :, 4:8, :] = own[d, i]
    for c in range(4):
        winds[c, :, 4:8, :] = edge[c].astype(jnp.float32)
        winds2[c, :, 4:8, :] = edge[4 + c].astype(jnp.float32)
    turbines[:, 4:8, :] = edge[8].astype(jnp.float32)

    def sides(low, high, low_edge, high_edge):
        for field in range(6):
            d, i = divmod(field, 3)
            tangents[field, :, 0:4, :] = low[d, i]
            tangents[field, :, 8:12, :] = high[d, i]
        for c in range(4):
            winds[c, :, 0:4, :] = low_edge[c].astype(jnp.float32)
            winds[c, :, 8:12, :] = high_edge[c].astype(jnp.float32)
        turbines[:, 0:4, :] = low_edge[8].astype(jnp.float32)
        turbines[:, 8:12, :] = high_edge[8].astype(jnp.float32)

    pl.when(place[4] == 0)(lambda: sides(other, mate, edge_other, edge_mate))
    pl.when(place[4] == 1)(lambda: sides(mate, other, edge_mate, edge_other))

    def level_rows(j, above, below):
        k = at(j)
        terms = wind_terms(winds, turbines, k, above, below, sign)
        rows = right_side(tangents, weights, terms, k, above, below)
        for c in range(2):
            power_out[c, k] = terms["turbine"] * terms["speed"] * terms["wind"][c]
        wind2 = [window(winds2, c, k) for c in range(2)]
        square = wind2[0] * wind2[0] + wind2[1] * wind2[1]
        scale = terms["turbine"] * (square * lax.rsqrt(square))
        return rows, [scale * wind2[0], scale * wind2[1]]

    def eliminate(j, above, below, carry):
        face_prev, ratio_prev, values_prev, face2_prev, ratio2_prev, w_prev = carry
        k = at(j)
        rows, wrows = level_rows(j, above, below)
        face = FACE * (window(winds, 3, k) + window(winds, 3, above))
        inverse = 1.0 / (1.0 + face + face_prev * (1.0 - ratio_prev))
        ratio = face * inverse
        values = [(r + face_prev * v) * inverse for r, v in zip(rows, values_prev)]
        ratio_out[k] = ratio
        for field in range(6):
            value_out[field, k] = values[field]
        face2 = FACE * (window(winds2, 3, k) + window(winds2, 3, above))
        inverse2 = 1.0 / (1.0 + face2 + face2_prev * (1.0 - ratio2_prev))
        ratio2 = face2 * inverse2
        ws = [(r + face2_prev * v) * inverse2 for r, v in zip(wrows, w_prev)]
        ratio2_out[k] = ratio2
        inverse2_out[k] = inverse2
        face2_out[k] = face2
        for c in range(2):
            wrow_out[c, k] = ws[c]
        return face, ratio, tuple(values), face2, ratio2, tuple(ws)

    zero = jnp.zeros((8, own.shape[4]), jnp.float32)
    carry = (
        (2.0 * FACE) * window(winds, 3, at(0)), zero, (zero,) * 6,
        (2.0 * FACE) * window(winds2, 3, at(0)), zero, (zero,) * 2,
    )
    carry = eliminate(0, at(1), None, carry)
    carry = lax.fori_loop(
        1, last, lambda j, c: eliminate(j, at(j + 1), at(j - 1), c), carry
    )
    face, ratio, values, face2, ratio2, ws = carry
    k = at(last)
    rows, wrows = level_rows(last, None, at(last - 1))
    for field in range(6):
        message[RHS + field] = rows[field] + face * values[field]
        message[RAW + field] = window(tangents, field, k)
    message[DIAG] = 1.0 + face * (1.0 - ratio)
    message[VISC] = window(winds, 3, k)
    message[DIAG2] = 1.0 + face2 * (1.0 - ratio2)
    message[VISC2] = window(winds2, 3, k)
    for c in range(3):
        message[WIND + c] = window(winds, c, k)
        message[WIND2 + c] = window(winds2, c, k)
    for c in range(2):
        message[WROW + c] = wrows[c] + face2 * ws[c]


def second_kernel(place, weights, mine, theirs, ratio_in, value_in, power_in, ratio2_in, inverse2_in,
                  face2_in, wrow_in, edge_mate, edge, edge_other,
                  row_out, value_out, middle_out, sums_out, tangents, winds, turbines, adjoint):
    levels = edge.shape[1]
    last = levels - 1
    sign = place[0].astype(jnp.float32)
    base = place[1]
    step = place[0]

    def at(j):
        return base + step * j

    for c in range(4):
        winds[c, :, 4:8, :] = edge[4 + c].astype(jnp.float32)
    turbines[:, 4:8, :] = edge[8].astype(jnp.float32)

    def sides(low_edge, high_edge):
        for c in range(3):
            winds[c, :, 0:4, :] = low_edge[4 + c].astype(jnp.float32)
            winds[c, :, 8:12, :] = high_edge[4 + c].astype(jnp.float32)

    pl.when(place[4] == 0)(lambda: sides(edge_other, edge_mate))
    pl.when(place[4] == 1)(lambda: sides(edge_mate, edge_other))

    zero = jnp.zeros((8, edge.shape[3]), jnp.float32)
    layer = lax.broadcasted_iota(jnp.int32, zero.shape, 0)
    inside = jnp.logical_and(layer >= place[2], layer < place[3])
    center = jnp.logical_and(layer >= 2, layer < 6)

    face = FACE * (mine[VISC] + theirs[VISC])
    pivot, pivot_far = mine[DIAG] + face, theirs[DIAG] + face
    inverse = 1.0 / (pivot * pivot_far - face * face)
    nexts, beyond = [], []
    for field in range(6):
        d, i = divmod(field, 3)
        row = mine[RHS + field] - (HALF * sign) * (
            mine[WIND + 2] * theirs[RAW + field] + mine[RAW + 3 * d + 2] * theirs[WIND + i]
        )
        row_far = theirs[RHS + field] + (HALF * sign) * (
            theirs[WIND + 2] * mine[RAW + field] + theirs[RAW + 3 * d + 2] * mine[WIND + i]
        )
        nexts.append(jnp.where(inside, (row * pivot_far + face * row_far) * inverse, 0.0))
        beyond.append(jnp.where(inside, (row_far * pivot + face * row) * inverse, 0.0))
    face2 = FACE * (mine[VISC2] + theirs[VISC2])
    pivot, pivot_far = mine[DIAG2] + face2, theirs[DIAG2] + face2
    inverse = 1.0 / (pivot * pivot_far - face2 * face2)
    near_part, far_part = pivot_far * inverse, face2 * inverse
    middle_out[0] = near_part
    middle_out[1] = far_part
    ws = [near_part * mine[WROW + c] + far_part * theirs[WROW + c] for c in range(2)]

    def keep(k, values, ws, sums):
        for field in range(6):
            tangents[field, k, 2:10, :] = values[field]
        for c in range(2):
            adjoint[c, k] = ws[c]
        return tuple(
            sums[d] + power_in[0, k] * values[3 * d] + power_in[1, k] * values[3 * d + 1]
            for d in range(2)
        )

    sums = keep(at(last), nexts, ws, (zero, zero))

    def back(n, carry):
        values, ws, sums = carry
        k = at(last - 1 - n)
        ratio = ratio_in[k]
        values = tuple(
            jnp.where(inside, value_in[f, k] + ratio * values[f], 0.0) for f in range(6)
        )
        ratio2 = ratio2_in[k]
        ws = tuple(wrow_in[c, k] + ratio2 * ws[c] for c in range(2))
        return values, ws, keep(k, values, ws, sums)

    _, _, sums = lax.fori_loop(0, last, back, (tuple(nexts), tuple(ws), sums))

    def level_rows(j, above, below, sums, winds_beyond=None, values_beyond=None):
        k = at(j)
        terms = wind_terms(winds, turbines, k, above, below, sign, winds_beyond)
        rows = right_side(tangents, weights, terms, k, above, below, values_beyond)
        sums = tuple(
            sums[d] + adjoint[0, k] * rows[3 * d] + adjoint[1, k] * rows[3 * d + 1]
            for d in range(2)
        )
        return rows, sums

    def eliminate(j, above, below, carry):
        face_prev, values_prev, sums = carry
        k = at(j)
        rows, sums = level_rows(j, above, below, sums)
        inverse = inverse2_in[k]
        values = tuple((r + face_prev * v) * inverse for r, v in zip(rows, values_prev))
        for field in range(6):
            value_out[field, k] = values[field]
        return face2_in[k], values, sums

    carry = eliminate(0, at(1), None, (zero, (zero,) * 6, sums))
    face, values, sums = lax.fori_loop(
        1, last, lambda j, c: eliminate(j, at(j + 1), at(j - 1), c), carry
    )
    rows, sums = level_rows(
        last, None, at(last - 1), sums, [theirs[WIND2 + c] for c in range(3)], beyond
    )
    for field in range(6):
        row_out[field] = rows[field] + face * values[field]
    for d in range(2):
        sums_out[d : d + 1, :] = jnp.sum(jnp.where(center, sums[d], 0.0), axis=0, keepdims=True)


def third_kernel(place, mine, theirs, middle, ratio_in, value_in, out):
    levels = ratio_in.shape[0]
    last = levels - 1
    base = place[1]
    step = place[0]
    values = tuple(middle[0] * mine[f] + middle[1] * theirs[f] for f in range(6))

    def keep(k, values):
        for field in range(6):
            d, i = divmod(field, 3)
            out[d, i, k] = values[field][2:6]

    keep(base + step * last, values)

    def back(n, values):
        k = base + step * (last - 1 - n)
        ratio = ratio_in[k]
        values = tuple(value_in[f, k] + ratio * values[f] for f in range(6))
        keep(k, values)
        return values

    lax.fori_loop(0, last, back, values)


def call(kernel, scalars, arrays, outs, scratch):
    return pl.pallas_call(
        kernel,
        out_shape=[jax.ShapeDtypeStruct(shape, jnp.float32) for shape in outs],
        in_specs=[pl.BlockSpec(memory_space=pltpu.SMEM)] * len(scalars)
        + [pl.BlockSpec(memory_space=pltpu.VMEM)] * len(arrays),
        out_specs=[pl.BlockSpec(memory_space=pltpu.VMEM)] * len(outs),
        scratch_shapes=[pltpu.VMEM(shape, jnp.float32) for shape in scratch],
        compiler_params=pltpu.CompilerParams(vmem_limit_bytes=40 * 1024 * 1024),
    )(*scalars, *arrays)


def prepare_kernel(slots, steps, records, code, first, second, arrived):
    per_device = records.shape[0]
    slot_a, slot_b = slots[steps[0]], slots[steps[1]]
    copy_a = pltpu.make_async_copy(records.at[lax.rem(slot_a, per_device)], first, arrived.at[0])
    copy_b = pltpu.make_async_copy(records.at[lax.rem(slot_b, per_device)], second, arrived.at[1])
    copy_a.start()
    copy_b.start()
    owners = slots.shape[0] // per_device
    code[0] = lax.div(slot_a, per_device) * owners + lax.div(slot_b, per_device)
    copy_a.wait()
    copy_b.wait()


def prepare(record_slot, step_record, records):
    block = jax.ShapeDtypeStruct(records.shape[1:], records.dtype)
    return pl.pallas_call(
        prepare_kernel,
        out_shape=[jax.ShapeDtypeStruct((1,), jnp.int32), block, block],
        in_specs=[pl.BlockSpec(memory_space=pltpu.SMEM)] * 2 + [pl.BlockSpec(memory_space=pl.ANY)],
        out_specs=[pl.BlockSpec(memory_space=pltpu.SMEM)] + [pl.BlockSpec(memory_space=pltpu.VMEM)] * 2,
        scratch_shapes=[pltpu.SemaphoreType.DMA((2,))],
    )(record_slot, step_record, records)


def swap_tiles(block):
    count = lax.axis_size("row")
    pairs = [(2 * i + 1, 2 * i + 2) for i in range(count - 1)]
    pairs += [(right, left) for left, right in pairs]
    return lax.ppermute(block, "core", [(0, 1), (1, 0)]), lax.ppermute(block, TILE, pairs)


def gather_inputs(code, first, second, tangent_in, mask):
    count = lax.axis_size("dir")
    here = lax.axis_index("dir")

    def send(record, owner):
        return [
            lax.ppermute(record, "dir", [(owner, (owner + k) % count)]) for k in range(1, count)
        ]

    def take(record, owner, got):
        for k, piece in enumerate(got, 1):
            record = jnp.where(here == (owner + k) % count, piece, record)
        return record

    def branch(a, b):
        def run(x, y, tangent, groups):
            got_a, got_b = send(x, a), send(y, b)
            tangents = swap_tiles(tangent)
            edge = jnp.concatenate(
                [take(x, a, got_a), take(y, b, got_b), groups.astype(x.dtype)[None]], axis=0
            )
            return edge, *tangents, *swap_tiles(edge)

        return run

    branches = [branch(a, b) for a in range(count) for b in range(count)]
    return lax.switch(code, branches, first, second, tangent_in, mask)


def shards(tangent_in, records, record_slot, step_record, turbine_mask, group_weights):
    directions, components, levels, layers, spans = tangent_in.shape
    fields = directions * components
    tiles = lax.axis_size("row") * lax.axis_size("core")
    tile = lax.axis_index("row") * lax.axis_size("core") + lax.axis_index("core")
    vert = lax.axis_index("vert")
    swap = [(0, 1), (1, 0)]

    code, first, second = prepare(record_slot, step_record, records)
    edge, mate, other, edge_mate, edge_other = gather_inputs(
        code[0], first, second, tangent_in, turbine_mask
    )

    place = jnp.stack([
        1 - 2 * vert,
        vert * (levels - 1),
        jnp.where(tile == 0, 2, 0),
        jnp.where(tile == tiles - 1, 6, 8),
        lax.axis_index("core"),
    ]).astype(jnp.int32)

    def block(*lead):
        return (*lead, 8, spans)

    def wide(*lead):
        return (*lead, 16, spans)

    message, ratio, value, power, ratio2, inverse2, face2, wrow = call(
        first_kernel,
        (place, group_weights),
        (mate, tangent_in, other, edge_mate, edge, edge_other),
        (block(FIELDS), block(levels), block(fields, levels), block(2, levels),
         block(levels), block(levels), block(levels), block(2, levels)),
        (wide(fields, levels), wide(4, levels), wide(4, levels), wide(levels)),
    )
    answer = lax.ppermute(message, "vert", swap)
    row, value2, middle, sums = call(
        second_kernel,
        (place, group_weights),
        (message, answer, ratio, value, power, ratio2, inverse2, face2, wrow, edge_mate, edge, edge_other),
        (block(fields), block(fields, levels), block(2), (directions, spans)),
        (wide(fields, levels), wide(4, levels), wide(levels), block(2, levels)),
    )
    answer2 = lax.ppermute(row, "vert", swap)

    sums = lax.psum(sums, "core")
    sums, answer2 = lax.optimization_barrier((sums, answer2))
    count = lax.axis_size("row") * lax.axis_size("vert")
    gathered = lax.all_to_all(
        jnp.broadcast_to(sums[None], (count, directions, spans)), ("row", "vert"), 0, 0, tiled=True
    )
    cells = levels * lax.axis_size("vert") * layers * tiles * spans
    power_out = jnp.sum(gathered, axis=(0, 2)) * (POWER_SCALE / math.sqrt(cells))

    (tangent_out,) = call(
        third_kernel,
        (place,),
        (row, answer2, middle, ratio2, value2),
        (tangent_in.shape,),
        (),
    )
    return tangent_out, power_out


def solution(mesh):
    tiles, verts, dirs = mesh.devices.shape
    fine = Mesh(mesh.devices.reshape(tiles // 2, 2, verts, dirs), (*TILE, "vert", "dir"))
    in_specs = (
        P("dir", None, "vert", TILE, None),
        P("dir", None, "vert", TILE, None),
        P(),
        P(),
        P("vert", TILE, None),
        P("dir", None),
    )
    out_specs = (P("dir", None, "vert", TILE, None), P("dir"))
    return jax.shard_map(shards, mesh=fine, in_specs=in_specs, out_specs=out_specs, check_vma=False)
```

```python
import functools
import math

import jax
import jax.numpy as jnp
from jax import lax
from jax.experimental import pallas as pl
from jax.experimental.pallas import tpu as pltpu
from jax.sharding import Mesh
from jax.sharding import PartitionSpec as P

STEPS = 2
TIME_STEP = 0.05
DRAG_COEFF = 0.5
POWER_SCALE = 0.01
VERTICAL_ASPECT = 400.0
TILE = ("row", "core")
UNROLL = 10
HALF = 0.5 * TIME_STEP
FACE = 0.5 * TIME_STEP * VERTICAL_ASPECT

RHS, DIAG, VISC, WIND, RAW, DIAG2, VISC2, WIND2, WROW, FIELDS = 0, 6, 7, 8, 11, 17, 18, 19, 22, 24


def window(ref, field, level, offset=0):
    return ref[field, level, 2 + offset : 10 + offset, :]


def roll_y(values, offset):
    return pltpu.roll(values, (-offset) % values.shape[-1], 1)


def wind_terms(winds, turbines, level, above, below, sign, beyond=None):
    wind = [window(winds, c, level) for c in range(3)]
    visc = TIME_STEP * window(winds, 3, level)
    mask = turbines[level, 2:10, :]
    turbine = jnp.where(mask > 0.5, 1.0, 0.0)
    square = wind[0] * wind[0] + wind[1] * wind[1]
    inverse = lax.rsqrt(square)
    speed = square * inverse
    drag = (DRAG_COEFF * TIME_STEP) * turbine
    along = drag * inverse
    by_first, by_second, by_third = [], [], []
    for c in range(3):
        near = window(winds, c, level, 1) - window(winds, c, level, -1)
        far = window(winds, c, level, 2) - window(winds, c, level, -2)
        slope = (TIME_STEP * 8.0 / 12.0) * near - (TIME_STEP / 12.0) * far
        by_first.append(slope + along * wind[c] * wind[0])
        near = roll_y(wind[c], 1) - roll_y(wind[c], -1)
        far = roll_y(wind[c], 2) - roll_y(wind[c], -2)
        slope = (TIME_STEP * 8.0 / 12.0) * near - (TIME_STEP / 12.0) * far
        by_second.append(slope + along * wind[c] * wind[1])
        vertical = jnp.zeros_like(speed)
        if beyond is not None:
            vertical = vertical + beyond[c]
        elif above is not None:
            vertical = vertical + window(winds, c, above)
        if below is not None:
            vertical = vertical - window(winds, c, below)
        by_third.append((HALF * sign) * vertical)
    first = (TIME_STEP * 8.0 / 12.0) * wind[0]
    second = (TIME_STEP * 8.0 / 12.0) * wind[1]
    return dict(
        wind=wind,
        mask=mask,
        turbine=turbine,
        speed=speed,
        center=1.0 - 4.0 * visc - drag * speed,
        x_up=visc - first,
        x_down=visc + first,
        x_far=0.125 * first,
        y_up=visc - second,
        y_down=visc + second,
        y_far=0.125 * second,
        z=(HALF * sign) * wind[2],
        by=(by_first, by_second, by_third),
    )


def right_side(tangents, weights, terms, level, above, below, beyond=None):
    speed_step = TIME_STEP * terms["speed"]
    groups = weights.shape[1]
    hits = [terms["mask"] == float(g + 1) for g in range(groups)]
    rows = []
    for d in range(weights.shape[0]):
        source = jnp.zeros_like(speed_step)
        for g in range(groups):
            source = jnp.where(hits[g], weights[d, g], source)
        force = source * speed_step
        own = [window(tangents, 3 * d + i, level) for i in range(3)]
        for i in range(3):
            field = 3 * d + i
            value = terms["center"] * own[i]
            value += terms["x_up"] * window(tangents, field, level, 1)
            value += terms["x_down"] * window(tangents, field, level, -1)
            value += terms["x_far"] * (
                window(tangents, field, level, 2) - window(tangents, field, level, -2)
            )
            value += terms["y_up"] * roll_y(own[i], 1)
            value += terms["y_down"] * roll_y(own[i], -1)
            value += terms["y_far"] * (roll_y(own[i], 2) - roll_y(own[i], -2))
            vertical = None
            if beyond is not None:
                vertical = beyond[field]
            elif above is not None:
                vertical = window(tangents, field, above)
            if below is not None:
                lower = window(tangents, field, below)
                vertical = -lower if vertical is None else vertical - lower
            if vertical is not None:
                value -= terms["z"] * vertical
            for c in range(3):
                value -= terms["by"][c][i] * own[c]
            value -= force * terms["wind"][i]
            rows.append(value)
    return rows


def first_kernel(place, weights, mate, own, other, edge_mate, edge, edge_other,
                 message, ratio_out, value_out, power_out, ratio2_out, inverse2_out, face2_out,
                 wrow_out, tangents, winds, winds2, turbines):
    levels = own.shape[2]
    last = levels - 1
    sign = place[0].astype(jnp.float32)
    base = place[1]
    step = place[0]

    def at(j):
        return base + step * j

    for field in range(6):
        d, i = divmod(field, 3)
        tangents[field, :, 4:8, :] = own[d, i]
    for c in range(4):
        winds[c, :, 4:8, :] = edge[c].astype(jnp.float32)
        winds2[c, :, 4:8, :] = edge[4 + c].astype(jnp.float32)
    turbines[:, 4:8, :] = edge[8].astype(jnp.float32)

    def sides(low, high, low_edge, high_edge):
        for field in range(6):
            d, i = divmod(field, 3)
            tangents[field, :, 0:4, :] = low[d, i]
            tangents[field, :, 8:12, :] = high[d, i]
        for c in range(4):
            winds[c, :, 0:4, :] = low_edge[c].astype(jnp.float32)
            winds[c, :, 8:12, :] = high_edge[c].astype(jnp.float32)
        turbines[:, 0:4, :] = low_edge[8].astype(jnp.float32)
        turbines[:, 8:12, :] = high_edge[8].astype(jnp.float32)

    pl.when(place[4] == 0)(lambda: sides(other, mate, edge_other, edge_mate))
    pl.when(place[4] == 1)(lambda: sides(mate, other, edge_mate, edge_other))

    def level_rows(j, above, below):
        k = at(j)
        terms = wind_terms(winds, turbines, k, above, below, sign)
        rows = right_side(tangents, weights, terms, k, above, below)
        for c in range(2):
            power_out[c, k] = terms["turbine"] * terms["speed"] * terms["wind"][c]
        wind2 = [window(winds2, c, k) for c in range(2)]
        square = wind2[0] * wind2[0] + wind2[1] * wind2[1]
        scale = terms["turbine"] * (square * lax.rsqrt(square))
        return rows, [scale * wind2[0], scale * wind2[1]]

    def eliminate(j, above, below, carry):
        face_prev, ratio_prev, values_prev, face2_prev, ratio2_prev, w_prev = carry
        k = at(j)
        rows, wrows = level_rows(j, above, below)
        face = FACE * (window(winds, 3, k) + window(winds, 3, above))
        inverse = 1.0 / (1.0 + face + face_prev * (1.0 - ratio_prev))
        ratio = face * inverse
        values = [(r + face_prev * v) * inverse for r, v in zip(rows, values_prev)]
        ratio_out[k] = ratio
        for field in range(6):
            value_out[field, k] = values[field]
        face2 = FACE * (window(winds2, 3, k) + window(winds2, 3, above))
        inverse2 = 1.0 / (1.0 + face2 + face2_prev * (1.0 - ratio2_prev))
        ratio2 = face2 * inverse2
        ws = [(r + face2_prev * v) * inverse2 for r, v in zip(wrows, w_prev)]
        ratio2_out[k] = ratio2
        inverse2_out[k] = inverse2
        face2_out[k] = face2
        for c in range(2):
            wrow_out[c, k] = ws[c]
        return face, ratio, tuple(values), face2, ratio2, tuple(ws)

    zero = jnp.zeros((8, own.shape[4]), jnp.float32)
    carry = (
        (2.0 * FACE) * window(winds, 3, at(0)), zero, (zero,) * 6,
        (2.0 * FACE) * window(winds2, 3, at(0)), zero, (zero,) * 2,
    )
    carry = eliminate(0, at(1), None, carry)
    carry = lax.fori_loop(
        1, last, lambda j, c: eliminate(j, at(j + 1), at(j - 1), c), carry, unroll=UNROLL
    )
    face, ratio, values, face2, ratio2, ws = carry
    k = at(last)
    rows, wrows = level_rows(last, None, at(last - 1))
    for field in range(6):
        message[RHS + field] = rows[field] + face * values[field]
        message[RAW + field] = window(tangents, field, k)
    message[DIAG] = 1.0 + face * (1.0 - ratio)
    message[VISC] = window(winds, 3, k)
    message[DIAG2] = 1.0 + face2 * (1.0 - ratio2)
    message[VISC2] = window(winds2, 3, k)
    for c in range(3):
        message[WIND + c] = window(winds, c, k)
        message[WIND2 + c] = window(winds2, c, k)
    for c in range(2):
        message[WROW + c] = wrows[c] + face2 * ws[c]


def second_kernel(place, weights, mine, theirs, ratio_in, value_in, power_in, ratio2_in, inverse2_in,
                  face2_in, wrow_in, edge_mate, edge, edge_other,
                  row_out, value_out, middle_out, sums_out, tangents, winds, turbines, adjoint):
    levels = edge.shape[1]
    last = levels - 1
    sign = place[0].astype(jnp.float32)
    base = place[1]
    step = place[0]

    def at(j):
        return base + step * j

    for c in range(4):
        winds[c, :, 4:8, :] = edge[4 + c].astype(jnp.float32)
    turbines[:, 4:8, :] = edge[8].astype(jnp.float32)

    def sides(low_edge, high_edge):
        for c in range(3):
            winds[c, :, 0:4, :] = low_edge[4 + c].astype(jnp.float32)
            winds[c, :, 8:12, :] = high_edge[4 + c].astype(jnp.float32)

    pl.when(place[4] == 0)(lambda: sides(edge_other, edge_mate))
    pl.when(place[4] == 1)(lambda: sides(edge_mate, edge_other))

    zero = jnp.zeros((8, edge.shape[3]), jnp.float32)
    layer = lax.broadcasted_iota(jnp.int32, zero.shape, 0)
    inside = jnp.logical_and(layer >= place[2], layer < place[3])
    center = jnp.logical_and(layer >= 2, layer < 6)

    face = FACE * (mine[VISC] + theirs[VISC])
    pivot, pivot_far = mine[DIAG] + face, theirs[DIAG] + face
    inverse = 1.0 / (pivot * pivot_far - face * face)
    nexts, beyond = [], []
    for field in range(6):
        d, i = divmod(field, 3)
        row = mine[RHS + field] - (HALF * sign) * (
            mine[WIND + 2] * theirs[RAW + field] + mine[RAW + 3 * d + 2] * theirs[WIND + i]
        )
        row_far = theirs[RHS + field] + (HALF * sign) * (
            theirs[WIND + 2] * mine[RAW + field] + theirs[RAW + 3 * d + 2] * mine[WIND + i]
        )
        nexts.append(jnp.where(inside, (row * pivot_far + face * row_far) * inverse, 0.0))
        beyond.append(jnp.where(inside, (row_far * pivot + face * row) * inverse, 0.0))
    face2 = FACE * (mine[VISC2] + theirs[VISC2])
    pivot, pivot_far = mine[DIAG2] + face2, theirs[DIAG2] + face2
    inverse = 1.0 / (pivot * pivot_far - face2 * face2)
    near_part, far_part = pivot_far * inverse, face2 * inverse
    middle_out[0] = near_part
    middle_out[1] = far_part
    ws = [near_part * mine[WROW + c] + far_part * theirs[WROW + c] for c in range(2)]

    def keep(k, values, ws, sums):
        for field in range(6):
            tangents[field, k, 2:10, :] = values[field]
        for c in range(2):
            adjoint[c, k] = ws[c]
        return tuple(
            sums[d] + power_in[0, k] * values[3 * d] + power_in[1, k] * values[3 * d + 1]
            for d in range(2)
        )

    sums = keep(at(last), nexts, ws, (zero, zero))

    def back(n, carry):
        values, ws, sums = carry
        k = at(last - 1 - n)
        ratio = ratio_in[k]
        values = tuple(
            jnp.where(inside, value_in[f, k] + ratio * values[f], 0.0) for f in range(6)
        )
        ratio2 = ratio2_in[k]
        ws = tuple(wrow_in[c, k] + ratio2 * ws[c] for c in range(2))
        return values, ws, keep(k, values, ws, sums)

    _, _, sums = lax.fori_loop(0, last, back, (tuple(nexts), tuple(ws), sums), unroll=True)

    def level_rows(j, above, below, sums, winds_beyond=None, values_beyond=None):
        k = at(j)
        terms = wind_terms(winds, turbines, k, above, below, sign, winds_beyond)
        rows = right_side(tangents, weights, terms, k, above, below, values_beyond)
        sums = tuple(
            sums[d] + adjoint[0, k] * rows[3 * d] + adjoint[1, k] * rows[3 * d + 1]
            for d in range(2)
        )
        return rows, sums

    def eliminate(j, above, below, carry):
        face_prev, values_prev, sums = carry
        k = at(j)
        rows, sums = level_rows(j, above, below, sums)
        inverse = inverse2_in[k]
        values = tuple((r + face_prev * v) * inverse for r, v in zip(rows, values_prev))
        for field in range(6):
            value_out[field, k] = values[field]
        return face2_in[k], values, sums

    carry = eliminate(0, at(1), None, (zero, (zero,) * 6, sums))
    face, values, sums = lax.fori_loop(
        1, last, lambda j, c: eliminate(j, at(j + 1), at(j - 1), c), carry, unroll=UNROLL
    )
    rows, sums = level_rows(
        last, None, at(last - 1), sums, [theirs[WIND2 + c] for c in range(3)], beyond
    )
    for field in range(6):
        row_out[field] = rows[field] + face * values[field]
    for d in range(2):
        sums_out[d : d + 1, :] = jnp.sum(jnp.where(center, sums[d], 0.0), axis=0, keepdims=True)


def third_kernel(place, mine, theirs, middle, ratio_in, value_in, out):
    levels = ratio_in.shape[0]
    last = levels - 1
    base = place[1]
    step = place[0]
    values = tuple(middle[0] * mine[f] + middle[1] * theirs[f] for f in range(6))

    def keep(k, values):
        for field in range(6):
            d, i = divmod(field, 3)
            out[d, i, k] = values[field][2:6]

    keep(base + step * last, values)

    def back(n, values):
        k = base + step * (last - 1 - n)
        ratio = ratio_in[k]
        values = tuple(value_in[f, k] + ratio * values[f] for f in range(6))
        keep(k, values)
        return values

    lax.fori_loop(0, last, back, values, unroll=True)


def call(kernel, scalars, arrays, outs, scratch):
    return pl.pallas_call(
        kernel,
        out_shape=[jax.ShapeDtypeStruct(shape, jnp.float32) for shape in outs],
        in_specs=[pl.BlockSpec(memory_space=pltpu.SMEM)] * len(scalars)
        + [pl.BlockSpec(memory_space=pltpu.VMEM)] * len(arrays),
        out_specs=[pl.BlockSpec(memory_space=pltpu.VMEM)] * len(outs),
        scratch_shapes=[pltpu.VMEM(shape, jnp.float32) for shape in scratch],
        compiler_params=pltpu.CompilerParams(vmem_limit_bytes=40 * 1024 * 1024),
    )(*scalars, *arrays)


def prepare_kernel(slots, steps, records, code, both, send, arrived):
    per_device, fields = records.shape[0], records.shape[1]
    owners = slots.shape[0] // per_device
    slot_a, slot_b = slots[steps[0]], slots[steps[1]]
    owner_b = lax.div(slot_b, per_device)
    chosen = jnp.where(lax.axis_index("dir") == owner_b, slot_b, slot_a)
    targets = (send, both.at[0:fields], both.at[fields : 2 * fields])
    copies = [
        pltpu.make_async_copy(records.at[lax.rem(slot, per_device)], target, arrived.at[n])
        for n, (slot, target) in enumerate(zip((chosen, slot_a, slot_b), targets))
    ]
    for copy in copies:
        copy.start()
    code[0] = lax.div(slot_a, per_device) * owners + owner_b
    for copy in copies:
        copy.wait()


def prepare(record_slot, step_record, records):
    fields, *block = records.shape[1:]
    shapes = [(2 * fields, *block), (fields, *block)]
    return pl.pallas_call(
        prepare_kernel,
        out_shape=[jax.ShapeDtypeStruct((1,), jnp.int32)]
        + [jax.ShapeDtypeStruct(shape, records.dtype) for shape in shapes],
        in_specs=[pl.BlockSpec(memory_space=pltpu.SMEM)] * 2 + [pl.BlockSpec(memory_space=pl.ANY)],
        out_specs=[pl.BlockSpec(memory_space=pltpu.SMEM)] + [pl.BlockSpec(memory_space=pltpu.VMEM)] * 2,
        scratch_shapes=[pltpu.SemaphoreType.DMA((3,))],
    )(record_slot, step_record, records)


def swap_tiles(block):
    count = lax.axis_size("row")
    pairs = [(2 * i + 1, 2 * i + 2) for i in range(count - 1)]
    pairs += [(right, left) for left, right in pairs]
    return lax.ppermute(block, "core", [(0, 1), (1, 0)]), lax.ppermute(block, TILE, pairs)


def gather_inputs(code, both, send, tangent_in, mask):
    count = lax.axis_size("dir")
    here = lax.axis_index("dir")
    fields = send.shape[0]

    def take(record, owner, got):
        for k, piece in enumerate(got, 1):
            record = jnp.where(here == (owner + k) % count, piece, record)
        return record

    def branch(a, b):
        def run(both, send, tangent, groups):
            block = both if a == b else send
            got = [
                lax.ppermute(block, "dir", [(o, (o + k) % count) for o in sorted({a, b})])
                for k in range(1, count)
            ]
            tangents = swap_tiles(tangent)
            if a == b:
                recs = [take(both, a, got)]
            else:
                recs = [take(both[:fields], a, got), take(both[fields:], b, got)]
            edge = jnp.concatenate([*recs, groups.astype(send.dtype)[None]], axis=0)
            return edge, *tangents, *swap_tiles(edge)

        return run

    branches = [branch(a, b) for a in range(count) for b in range(count)]
    return lax.switch(code, branches, both, send, tangent_in, mask)


def shards(tangent_in, records, record_slot, step_record, turbine_mask, group_weights):
    directions, components, levels, layers, spans = tangent_in.shape
    fields = directions * components
    tiles = lax.axis_size("row") * lax.axis_size("core")
    tile = lax.axis_index("row") * lax.axis_size("core") + lax.axis_index("core")
    vert = lax.axis_index("vert")
    swap = [(0, 1), (1, 0)]

    place = jnp.stack([
        1 - 2 * vert,
        vert * (levels - 1),
        jnp.where(tile == 0, 2, 0),
        jnp.where(tile == tiles - 1, 6, 8),
        lax.axis_index("core"),
    ]).astype(jnp.int32)

    code, both, send = prepare(record_slot, step_record, records)
    edge, mate, other, edge_mate, edge_other = gather_inputs(
        code[0], both, send, tangent_in, turbine_mask
    )

    def block(*lead):
        return (*lead, 8, spans)

    def wide(*lead):
        return (*lead, 16, spans)

    message, ratio, value, power, ratio2, inverse2, face2, wrow = call(
        first_kernel,
        (place, group_weights),
        (mate, tangent_in, other, edge_mate, edge, edge_other),
        (block(FIELDS), block(levels), block(fields, levels), block(2, levels),
         block(levels), block(levels), block(levels), block(2, levels)),
        (wide(fields, levels), wide(4, levels), wide(4, levels), wide(levels)),
    )
    answer = lax.ppermute(message, "vert", swap)
    row, value2, middle, sums = call(
        second_kernel,
        (place, group_weights),
        (message, answer, ratio, value, power, ratio2, inverse2, face2, wrow, edge_mate, edge, edge_other),
        (block(fields), block(fields, levels), block(2), (directions, spans)),
        (wide(fields, levels), wide(4, levels), wide(levels), block(2, levels)),
    )
    answer2 = lax.ppermute(row, "vert", swap)

    sums = lax.psum(sums, "core")
    sums, answer2 = lax.optimization_barrier((sums, answer2))
    count = lax.axis_size("row") * lax.axis_size("vert")
    gathered = lax.all_to_all(
        jnp.broadcast_to(sums[None], (count, directions, spans)), ("row", "vert"), 0, 0, tiled=True
    )
    cells = levels * lax.axis_size("vert") * layers * tiles * spans
    power_out = jnp.sum(gathered, axis=(0, 2)) * (POWER_SCALE / math.sqrt(cells))

    (tangent_out,) = call(
        third_kernel,
        (place,),
        (row, answer2, middle, ratio2, value2),
        (tangent_in.shape,),
        (),
    )
    return tangent_out, power_out


def solution(mesh):
    tiles, verts, dirs = mesh.devices.shape
    fine = Mesh(mesh.devices.reshape(tiles // 2, 2, verts, dirs), (*TILE, "vert", "dir"))
    in_specs = (
        P("dir", None, "vert", TILE, None),
        P("dir", None, "vert", TILE, None),
        P(),
        P(),
        P("vert", TILE, None),
        P("dir", None),
    )
    out_specs = (P("dir", None, "vert", TILE, None), P("dir"))
    return jax.shard_map(shards, mesh=fine, in_specs=in_specs, out_specs=out_specs, check_vma=False)
```

```python
import functools
import math

import jax
import jax.numpy as jnp
from jax import lax
from jax.experimental import pallas as pl
from jax.experimental.pallas import tpu as pltpu
from jax.sharding import Mesh
from jax.sharding import PartitionSpec as P

STEPS = 2
TIME_STEP = 0.05
DRAG_COEFF = 0.5
POWER_SCALE = 0.01
VERTICAL_ASPECT = 400.0
TILE = ("row", "core")
UNROLL = 10
HALF = 0.5 * TIME_STEP
FACE = 0.5 * TIME_STEP * VERTICAL_ASPECT

RHS, DIAG, VISC, WIND, RAW, DIAG2, VISC2, WIND2, WROW, FIELDS = 0, 6, 7, 8, 11, 17, 18, 19, 22, 24


def window(ref, field, level, offset=0):
    return ref[field, level, 2 + offset : 10 + offset, :]


def roll_y(values, offset):
    return pltpu.roll(values, (-offset) % values.shape[-1], 1)


def wind_terms(winds, turbines, weights, level, above, below, sign):
    wind = [window(winds, c, level) for c in range(3)]
    visc = TIME_STEP * window(winds, 3, level)
    mask = turbines[level, 2:10, :]
    turbine = jnp.where(mask > 0.5, 1.0, 0.0)
    square = wind[0] * wind[0] + wind[1] * wind[1]
    inverse = lax.rsqrt(square)
    speed = square * inverse
    drag = (DRAG_COEFF * TIME_STEP) * turbine
    along = drag * inverse
    by_first, by_second, by_third = [], [], []
    for c in range(3):
        near = window(winds, c, level, 1) - window(winds, c, level, -1)
        far = window(winds, c, level, 2) - window(winds, c, level, -2)
        slope = (TIME_STEP * 8.0 / 12.0) * near - (TIME_STEP / 12.0) * far
        by_first.append(slope + along * wind[c] * wind[0])
        near = roll_y(wind[c], 1) - roll_y(wind[c], -1)
        far = roll_y(wind[c], 2) - roll_y(wind[c], -2)
        slope = (TIME_STEP * 8.0 / 12.0) * near - (TIME_STEP / 12.0) * far
        by_second.append(slope + along * wind[c] * wind[1])
        vertical = jnp.zeros_like(speed)
        if above is not None:
            vertical = vertical + window(winds, c, above)
        if below is not None:
            vertical = vertical - window(winds, c, below)
        by_third.append((HALF * sign) * vertical)
    speed_step = TIME_STEP * speed
    force = []
    for d in range(weights.shape[0]):
        source = jnp.zeros_like(speed_step)
        for g in range(weights.shape[1]):
            source = jnp.where(mask == float(g + 1), weights[d, g], source)
        force.append(source * speed_step)
    first = (TIME_STEP * 8.0 / 12.0) * wind[0]
    second = (TIME_STEP * 8.0 / 12.0) * wind[1]
    return dict(
        wind=wind,
        force=force,
        turbine=turbine,
        speed=speed,
        center=1.0 - 4.0 * visc - drag * speed,
        x_up=visc - first,
        x_down=visc + first,
        x_far=0.125 * first,
        y_up=visc - second,
        y_down=visc + second,
        y_far=0.125 * second,
        z=(HALF * sign) * wind[2],
        by=(by_first, by_second, by_third),
    )


def right_side(tangents, terms, level, above, below, beyond=None):
    rows = []
    for d, force in enumerate(terms["force"]):
        own = [window(tangents, 3 * d + i, level) for i in range(3)]
        for i in range(3):
            field = 3 * d + i
            value = terms["center"] * own[i]
            value += terms["x_up"] * window(tangents, field, level, 1)
            value += terms["x_down"] * window(tangents, field, level, -1)
            value += terms["x_far"] * (
                window(tangents, field, level, 2) - window(tangents, field, level, -2)
            )
            value += terms["y_up"] * roll_y(own[i], 1)
            value += terms["y_down"] * roll_y(own[i], -1)
            value += terms["y_far"] * (roll_y(own[i], 2) - roll_y(own[i], -2))
            vertical = None
            if beyond is not None:
                vertical = beyond[field]
            elif above is not None:
                vertical = window(tangents, field, above)
            if below is not None:
                lower = window(tangents, field, below)
                vertical = -lower if vertical is None else vertical - lower
            if vertical is not None:
                value -= terms["z"] * vertical
            for c in range(3):
                value -= terms["by"][c][i] * own[c]
            value -= force * terms["wind"][i]
            rows.append(value)
    return rows


def first_kernel(place, weights, mate, own, other, edge_mate, edge, edge_other,
                 message, ratio_out, value_out, power_out, ratio2_out, inverse2_out, face2_out,
                 wrow_out, tangents, winds, winds2, turbines):
    levels = own.shape[2]
    last = levels - 1
    sign = place[0].astype(jnp.float32)
    base = place[1]
    step = place[0]

    def at(j):
        return base + step * j

    for field in range(6):
        d, i = divmod(field, 3)
        tangents[field, :, 4:8, :] = own[d, i]
    for c in range(4):
        winds[c, :, 4:8, :] = edge[c].astype(jnp.float32)
        winds2[c, :, 4:8, :] = edge[4 + c].astype(jnp.float32)
    turbines[:, 4:8, :] = edge[8].astype(jnp.float32)

    def sides(low, high, low_edge, high_edge):
        for field in range(6):
            d, i = divmod(field, 3)
            tangents[field, :, 0:4, :] = low[d, i]
            tangents[field, :, 8:12, :] = high[d, i]
        for c in range(4):
            winds[c, :, 0:4, :] = low_edge[c].astype(jnp.float32)
            winds[c, :, 8:12, :] = high_edge[c].astype(jnp.float32)
        turbines[:, 0:4, :] = low_edge[8].astype(jnp.float32)
        turbines[:, 8:12, :] = high_edge[8].astype(jnp.float32)

    pl.when(place[4] == 0)(lambda: sides(other, mate, edge_other, edge_mate))
    pl.when(place[4] == 1)(lambda: sides(mate, other, edge_mate, edge_other))

    def level_rows(j, above, below):
        k = at(j)
        terms = wind_terms(winds, turbines, weights, k, above, below, sign)
        rows = right_side(tangents, terms, k, above, below)
        for c in range(2):
            power_out[c, k] = terms["turbine"] * terms["speed"] * terms["wind"][c]
        wind2 = [window(winds2, c, k) for c in range(2)]
        square = wind2[0] * wind2[0] + wind2[1] * wind2[1]
        scale = terms["turbine"] * (square * lax.rsqrt(square))
        return rows, [scale * wind2[0], scale * wind2[1]]

    def eliminate(j, above, below, carry):
        face_prev, ratio_prev, values_prev, face2_prev, ratio2_prev, w_prev = carry
        k = at(j)
        rows, wrows = level_rows(j, above, below)
        face = FACE * (window(winds, 3, k) + window(winds, 3, above))
        inverse = 1.0 / (1.0 + face + face_prev * (1.0 - ratio_prev))
        ratio = face * inverse
        values = [(r + face_prev * v) * inverse for r, v in zip(rows, values_prev)]
        ratio_out[k] = ratio
        for field in range(6):
            value_out[field, k] = values[field]
        face2 = FACE * (window(winds2, 3, k) + window(winds2, 3, above))
        inverse2 = 1.0 / (1.0 + face2 + face2_prev * (1.0 - ratio2_prev))
        ratio2 = face2 * inverse2
        ws = [(r + face2_prev * v) * inverse2 for r, v in zip(wrows, w_prev)]
        ratio2_out[k] = ratio2
        inverse2_out[k] = inverse2
        face2_out[k] = face2
        for c in range(2):
            wrow_out[c, k] = ws[c]
        return face, ratio, tuple(values), face2, ratio2, tuple(ws)

    zero = jnp.zeros((8, own.shape[4]), jnp.float32)
    carry = (
        (2.0 * FACE) * window(winds, 3, at(0)), zero, (zero,) * 6,
        (2.0 * FACE) * window(winds2, 3, at(0)), zero, (zero,) * 2,
    )
    carry = eliminate(0, at(1), None, carry)
    carry = lax.fori_loop(
        1, last, lambda j, c: eliminate(j, at(j + 1), at(j - 1), c), carry, unroll=UNROLL
    )
    face, ratio, values, face2, ratio2, ws = carry
    k = at(last)
    rows, wrows = level_rows(last, None, at(last - 1))
    for field in range(6):
        message[RHS + field] = rows[field] + face * values[field]
        message[RAW + field] = window(tangents, field, k)
    message[DIAG] = 1.0 + face * (1.0 - ratio)
    message[VISC] = window(winds, 3, k)
    message[DIAG2] = 1.0 + face2 * (1.0 - ratio2)
    message[VISC2] = window(winds2, 3, k)
    for c in range(3):
        message[WIND + c] = window(winds, c, k)
        message[WIND2 + c] = window(winds2, c, k)
    for c in range(2):
        message[WROW + c] = wrows[c] + face2 * ws[c]


SINGLE = ("center", "x_up", "x_down", "x_far", "y_up", "y_down", "y_far", "z")
TERMS = len(SINGLE) + 3 + 9


def terms_kernel(place, weights, edge_mate, edge, edge_other, out, winds, turbines):
    levels = edge.shape[1]
    last = levels - 1
    sign = place[0].astype(jnp.float32)
    base = place[1]
    step = place[0]
    directions = weights.shape[0]

    def at(j):
        return base + step * j

    for c in range(4):
        winds[c, :, 4:8, :] = edge[4 + c].astype(jnp.float32)
    turbines[:, 4:8, :] = edge[8].astype(jnp.float32)

    def sides(low_edge, high_edge):
        for c in range(3):
            winds[c, :, 0:4, :] = low_edge[4 + c].astype(jnp.float32)
            winds[c, :, 8:12, :] = high_edge[4 + c].astype(jnp.float32)

    pl.when(place[4] == 0)(lambda: sides(edge_other, edge_mate))
    pl.when(place[4] == 1)(lambda: sides(edge_mate, edge_other))

    def level_terms(j, above, below):
        k = at(j)
        terms = wind_terms(winds, turbines, weights, k, above, below, sign)
        values = [terms[name] for name in SINGLE] + terms["wind"] + terms["force"]
        for part in terms["by"]:
            values += part
        for n, value in enumerate(values):
            out[n, k] = value

    level_terms(0, at(1), None)

    def body(j, carry):
        level_terms(j, at(j + 1), at(j - 1))
        return carry

    lax.fori_loop(1, last, body, 0, unroll=UNROLL)
    level_terms(last, None, at(last - 1))


def stored_terms(store, level):
    terms = {name: store[n, level] for n, name in enumerate(SINGLE)}
    start = len(SINGLE)
    terms["wind"] = [store[start + i, level] for i in range(3)]
    count = store.shape[0] - TERMS
    terms["force"] = [store[start + 3 + d, level] for d in range(count)]
    start += 3 + count
    terms["by"] = [[store[start + 3 * c + i, level] for i in range(3)] for c in range(3)]
    return terms


def second_kernel(scale, place, mine, theirs, ratio_in, value_in, power_in, ratio2_in, inverse2_in,
                  face2_in, wrow_in, store,
                  row_out, value_out, middle_out, sums_out, tangents, adjoint):
    levels = ratio_in.shape[0]
    last = levels - 1
    sign = place[0].astype(jnp.float32)
    base = place[1]
    step = place[0]

    def at(j):
        return base + step * j

    zero = jnp.zeros(ratio_in.shape[1:], jnp.float32)
    layer = lax.broadcasted_iota(jnp.int32, zero.shape, 0)
    inside = jnp.logical_and(layer >= place[2], layer < place[3])
    center = jnp.logical_and(layer >= 2, layer < 6)

    face = FACE * (mine[VISC] + theirs[VISC])
    pivot, pivot_far = mine[DIAG] + face, theirs[DIAG] + face
    inverse = 1.0 / (pivot * pivot_far - face * face)
    nexts, beyond = [], []
    for field in range(6):
        d, i = divmod(field, 3)
        row = mine[RHS + field] - (HALF * sign) * (
            mine[WIND + 2] * theirs[RAW + field] + mine[RAW + 3 * d + 2] * theirs[WIND + i]
        )
        row_far = theirs[RHS + field] + (HALF * sign) * (
            theirs[WIND + 2] * mine[RAW + field] + theirs[RAW + 3 * d + 2] * mine[WIND + i]
        )
        nexts.append(jnp.where(inside, (row * pivot_far + face * row_far) * inverse, 0.0))
        beyond.append(jnp.where(inside, (row_far * pivot + face * row) * inverse, 0.0))
    face2 = FACE * (mine[VISC2] + theirs[VISC2])
    pivot, pivot_far = mine[DIAG2] + face2, theirs[DIAG2] + face2
    inverse = 1.0 / (pivot * pivot_far - face2 * face2)
    near_part, far_part = pivot_far * inverse, face2 * inverse
    middle_out[0] = near_part
    middle_out[1] = far_part
    ws = [near_part * mine[WROW + c] + far_part * theirs[WROW + c] for c in range(2)]

    def keep(k, values, ws, sums):
        for field in range(6):
            tangents[field, k, 2:10, :] = values[field]
        for c in range(2):
            adjoint[c, k] = ws[c]
        return tuple(
            sums[d] + power_in[0, k] * values[3 * d] + power_in[1, k] * values[3 * d + 1]
            for d in range(2)
        )

    sums = keep(at(last), nexts, ws, (zero, zero))

    def back(n, carry):
        values, ws, sums = carry
        k = at(last - 1 - n)
        ratio = ratio_in[k]
        values = tuple(
            jnp.where(inside, value_in[f, k] + ratio * values[f], 0.0) for f in range(6)
        )
        ratio2 = ratio2_in[k]
        ws = tuple(wrow_in[c, k] + ratio2 * ws[c] for c in range(2))
        return values, ws, keep(k, values, ws, sums)

    _, _, sums = lax.fori_loop(0, last, back, (tuple(nexts), tuple(ws), sums), unroll=True)

    def level_rows(j, above, below, sums, values_beyond=None):
        k = at(j)
        terms = stored_terms(store, k)
        if values_beyond is not None:
            for i in range(3):
                terms["by"][2][i] += (HALF * sign) * theirs[WIND2 + i]
        rows = right_side(tangents, terms, k, above, below, values_beyond)
        sums = tuple(
            sums[d] + adjoint[0, k] * rows[3 * d] + adjoint[1, k] * rows[3 * d + 1]
            for d in range(2)
        )
        return rows, sums

    def eliminate(j, above, below, carry):
        face_prev, values_prev, sums = carry
        k = at(j)
        rows, sums = level_rows(j, above, below, sums)
        inverse = inverse2_in[k]
        values = tuple((r + face_prev * v) * inverse for r, v in zip(rows, values_prev))
        for field in range(6):
            value_out[field, k] = values[field]
        return face2_in[k], values, sums

    carry = eliminate(0, at(1), None, (zero, (zero,) * 6, sums))
    face, values, sums = lax.fori_loop(
        1, last, lambda j, c: eliminate(j, at(j + 1), at(j - 1), c), carry, unroll=UNROLL
    )
    rows, sums = level_rows(last, None, at(last - 1), sums, beyond)
    for field in range(6):
        row_out[field] = rows[field] + face * values[field]
    for d in range(2):
        sums_out[d : d + 1, :] = scale * jnp.sum(
            jnp.where(center, sums[d], 0.0), axis=0, keepdims=True
        )


def third_kernel(place, mine, theirs, middle, ratio_in, value_in, out):
    levels = ratio_in.shape[0]
    last = levels - 1
    base = place[1]
    step = place[0]
    values = tuple(middle[0] * mine[f] + middle[1] * theirs[f] for f in range(6))

    def keep(k, values):
        for field in range(6):
            d, i = divmod(field, 3)
            out[d, i, k] = values[field][2:6]

    keep(base + step * last, values)

    def back(n, values):
        k = base + step * (last - 1 - n)
        ratio = ratio_in[k]
        values = tuple(value_in[f, k] + ratio * values[f] for f in range(6))
        keep(k, values)
        return values

    lax.fori_loop(0, last, back, values, unroll=True)


def call(kernel, scalars, arrays, outs, scratch):
    return pl.pallas_call(
        kernel,
        out_shape=[jax.ShapeDtypeStruct(shape, jnp.float32) for shape in outs],
        in_specs=[pl.BlockSpec(memory_space=pltpu.SMEM)] * len(scalars)
        + [pl.BlockSpec(memory_space=pltpu.VMEM)] * len(arrays),
        out_specs=[pl.BlockSpec(memory_space=pltpu.VMEM)] * len(outs),
        scratch_shapes=[pltpu.VMEM(shape, jnp.float32) for shape in scratch],
        compiler_params=pltpu.CompilerParams(vmem_limit_bytes=40 * 1024 * 1024),
    )(*scalars, *arrays)


def prepare_kernel(slots, steps, records, groups, code, both, send, mask, groups_here, arrived):
    per_device, fields = records.shape[0], records.shape[1]
    owners = slots.shape[0] // per_device
    slot_a, slot_b = slots[steps[0]], slots[steps[1]]
    owner_b = lax.div(slot_b, per_device)
    chosen = jnp.where(lax.axis_index("dir") == owner_b, slot_b, slot_a)
    targets = (send, both.at[0:fields], both.at[fields : 2 * fields])
    copies = [
        pltpu.make_async_copy(records.at[lax.rem(slot, per_device)], target, arrived.at[n])
        for n, (slot, target) in enumerate(zip((chosen, slot_a, slot_b), targets))
    ]
    copies.append(pltpu.make_async_copy(groups, groups_here, arrived.at[3]))
    for copy in copies:
        copy.start()
    code[0] = lax.div(slot_a, per_device) * owners + owner_b
    copies[3].wait()
    mask[0] = groups_here[...].astype(jnp.float32).astype(mask.dtype)
    for copy in copies[:3]:
        copy.wait()


def prepare(record_slot, step_record, records, turbine_mask):
    fields, *block = records.shape[1:]
    shapes = [(2 * fields, *block), (fields, *block), (1, *block)]
    return pl.pallas_call(
        prepare_kernel,
        out_shape=[jax.ShapeDtypeStruct((1,), jnp.int32)]
        + [jax.ShapeDtypeStruct(shape, records.dtype) for shape in shapes],
        in_specs=[pl.BlockSpec(memory_space=pltpu.SMEM)] * 2 + [pl.BlockSpec(memory_space=pl.ANY)] * 2,
        out_specs=[pl.BlockSpec(memory_space=pltpu.SMEM)] + [pl.BlockSpec(memory_space=pltpu.VMEM)] * 3,
        scratch_shapes=[
            pltpu.VMEM(turbine_mask.shape, turbine_mask.dtype),
            pltpu.SemaphoreType.DMA((4,)),
        ],
    )(record_slot, step_record, records, turbine_mask)


def swap_tiles(block):
    count = lax.axis_size("row")
    pairs = [(2 * i + 1, 2 * i + 2) for i in range(count - 1)]
    pairs += [(right, left) for left, right in pairs]
    return lax.ppermute(block, "core", [(0, 1), (1, 0)]), lax.ppermute(block, TILE, pairs)


def gather_inputs(code, both, send, tangent_in, mask):
    count = lax.axis_size("dir")
    here = lax.axis_index("dir")
    fields = send.shape[0]

    def take(record, owner, got):
        for k, piece in enumerate(got, 1):
            record = jnp.where(here == (owner + k) % count, piece, record)
        return record

    def branch(a, b):
        def run(both, send, tangent, mask):
            block = both if a == b else send
            got = [
                lax.ppermute(block, "dir", [(o, (o + k) % count) for o in sorted({a, b})])
                for k in range(1, count)
            ]
            tangents = swap_tiles(tangent)
            if a == b:
                recs = [take(both, a, got)]
            else:
                recs = [take(both[:fields], a, got), take(both[fields:], b, got)]
            edge = jnp.concatenate([*recs, mask], axis=0)
            return edge, *tangents, *swap_tiles(edge)

        return run

    branches = [branch(a, b) for a in range(count) for b in range(count)]
    return lax.switch(code, branches, both, send, tangent_in, mask)


def shards(tangent_in, records, record_slot, step_record, turbine_mask, group_weights):
    directions, components, levels, layers, spans = tangent_in.shape
    fields = directions * components
    tiles = lax.axis_size("row") * lax.axis_size("core")
    tile = lax.axis_index("row") * lax.axis_size("core") + lax.axis_index("core")
    vert = lax.axis_index("vert")
    swap = [(0, 1), (1, 0)]

    place = jnp.stack([
        1 - 2 * vert,
        vert * (levels - 1),
        jnp.where(tile == 0, 2, 0),
        jnp.where(tile == tiles - 1, 6, 8),
        lax.axis_index("core"),
    ]).astype(jnp.int32)

    code, both, send, mask = prepare(record_slot, step_record, records, turbine_mask)
    edge, mate, other, edge_mate, edge_other = gather_inputs(
        code[0], both, send, tangent_in, mask
    )

    def block(*lead):
        return (*lead, 8, spans)

    def wide(*lead):
        return (*lead, 16, spans)

    message, ratio, value, power, ratio2, inverse2, face2, wrow = call(
        first_kernel,
        (place, group_weights),
        (mate, tangent_in, other, edge_mate, edge, edge_other),
        (block(FIELDS), block(levels), block(fields, levels), block(2, levels),
         block(levels), block(levels), block(levels), block(2, levels)),
        (wide(fields, levels), wide(4, levels), wide(4, levels), wide(levels)),
    )
    answer = lax.ppermute(message, "vert", swap)
    (store,) = call(
        terms_kernel,
        (place, group_weights),
        (edge_mate, edge, edge_other),
        (block(TERMS + directions, levels),),
        (wide(4, levels), wide(levels)),
    )
    cells = levels * lax.axis_size("vert") * layers * tiles * spans
    row, value2, middle, sums = call(
        functools.partial(second_kernel, POWER_SCALE / math.sqrt(cells)),
        (place,),
        (message, answer, ratio, value, power, ratio2, inverse2, face2, wrow, store),
        (block(fields), block(fields, levels), block(2), (directions, spans)),
        (wide(fields, levels), block(2, levels)),
    )
    answer2 = lax.ppermute(row, "vert", swap)

    sums = lax.psum(sums, "core")
    count = lax.axis_size("row") * lax.axis_size("vert")
    gathered = lax.all_to_all(
        jnp.broadcast_to(sums[None], (count, directions, spans)), ("row", "vert"), 0, 0, tiled=True
    )
    power_out = jnp.sum(gathered, axis=(0, 2))

    (tangent_out,) = call(
        third_kernel,
        (place,),
        (row, answer2, middle, ratio2, value2),
        (tangent_in.shape,),
        (),
    )
    return tangent_out, power_out


def solution(mesh):
    tiles, verts, dirs = mesh.devices.shape
    fine = Mesh(mesh.devices.reshape(tiles // 2, 2, verts, dirs), (*TILE, "vert", "dir"))
    in_specs = (
        P("dir", None, "vert", TILE, None),
        P("dir", None, "vert", TILE, None),
        P(),
        P(),
        P("vert", TILE, None),
        P("dir", None),
    )
    out_specs = (P("dir", None, "vert", TILE, None), P("dir"))
    return jax.shard_map(shards, mesh=fine, in_specs=in_specs, out_specs=out_specs, check_vma=False)
```

```python
import functools
import math

import jax
import jax.numpy as jnp
from jax import lax
from jax.experimental import pallas as pl
from jax.experimental.pallas import tpu as pltpu
from jax.sharding import Mesh
from jax.sharding import PartitionSpec as P

STEPS = 2
TIME_STEP = 0.05
DRAG_COEFF = 0.5
POWER_SCALE = 0.01
VERTICAL_ASPECT = 400.0
TILE = ("row", "core")
UNROLL = 10
HALF = 0.5 * TIME_STEP
FACE = 0.5 * TIME_STEP * VERTICAL_ASPECT

RHS, DIAG, VISC, WIND, RAW, DIAG2, VISC2, WIND2, WROW, FIELDS = 0, 6, 7, 8, 11, 17, 18, 19, 22, 24


def window(ref, field, level, offset=0):
    return ref[field, level, 8 + offset : 16 + offset, :]


def roll_y(values, offset):
    return pltpu.roll(values, (-offset) % values.shape[-1], 1)


def wind_terms(winds, turbines, weights, level, above, below, sign):
    wind = [window(winds, c, level) for c in range(3)]
    visc = TIME_STEP * window(winds, 3, level)
    mask = turbines[level, 8:16, :]
    turbine = jnp.where(mask > 0.5, 1.0, 0.0)
    square = wind[0] * wind[0] + wind[1] * wind[1]
    inverse = lax.rsqrt(square)
    speed = square * inverse
    drag = (DRAG_COEFF * TIME_STEP) * turbine
    along = drag * inverse
    by_first, by_second, by_third = [], [], []
    for c in range(3):
        near = window(winds, c, level, 1) - window(winds, c, level, -1)
        far = window(winds, c, level, 2) - window(winds, c, level, -2)
        slope = (TIME_STEP * 8.0 / 12.0) * near - (TIME_STEP / 12.0) * far
        by_first.append(slope + along * wind[c] * wind[0])
        near = roll_y(wind[c], 1) - roll_y(wind[c], -1)
        far = roll_y(wind[c], 2) - roll_y(wind[c], -2)
        slope = (TIME_STEP * 8.0 / 12.0) * near - (TIME_STEP / 12.0) * far
        by_second.append(slope + along * wind[c] * wind[1])
        vertical = jnp.zeros_like(speed)
        if above is not None:
            vertical = vertical + window(winds, c, above)
        if below is not None:
            vertical = vertical - window(winds, c, below)
        by_third.append((HALF * sign) * vertical)
    speed_step = TIME_STEP * speed
    force = []
    for d in range(weights.shape[0]):
        source = jnp.zeros_like(speed_step)
        for g in range(weights.shape[1]):
            source = jnp.where(mask == float(g + 1), weights[d, g], source)
        force.append(source * speed_step)
    first = (TIME_STEP * 8.0 / 12.0) * wind[0]
    second = (TIME_STEP * 8.0 / 12.0) * wind[1]
    return dict(
        wind=wind,
        force=force,
        turbine=turbine,
        speed=speed,
        center=1.0 - 4.0 * visc - drag * speed,
        x_up=visc - first,
        x_down=visc + first,
        x_far=0.125 * first,
        y_up=visc - second,
        y_down=visc + second,
        y_far=0.125 * second,
        z=(HALF * sign) * wind[2],
        by=(by_first, by_second, by_third),
    )


def right_side(tangents, terms, level, above, below, beyond=None):
    rows = []
    for d, force in enumerate(terms["force"]):
        own = [window(tangents, 3 * d + i, level) for i in range(3)]
        for i in range(3):
            field = 3 * d + i
            value = terms["center"] * own[i]
            value += terms["x_up"] * window(tangents, field, level, 1)
            value += terms["x_down"] * window(tangents, field, level, -1)
            value += terms["x_far"] * (
                window(tangents, field, level, 2) - window(tangents, field, level, -2)
            )
            value += terms["y_up"] * roll_y(own[i], 1)
            value += terms["y_down"] * roll_y(own[i], -1)
            value += terms["y_far"] * (roll_y(own[i], 2) - roll_y(own[i], -2))
            vertical = None
            if beyond is not None:
                vertical = beyond[field]
            elif above is not None:
                vertical = window(tangents, field, above)
            if below is not None:
                lower = window(tangents, field, below)
                vertical = -lower if vertical is None else vertical - lower
            if vertical is not None:
                value -= terms["z"] * vertical
            for c in range(3):
                value -= terms["by"][c][i] * own[c]
            value -= force * terms["wind"][i]
            rows.append(value)
    return rows


def first_kernel(place, weights, mate, own, other, edge_mate, edge, edge_other, visc,
                 message, ratio_out, value_out, power_out, ratio2_out, inverse2_out, face2_out,
                 wrow_out, tangents, winds, winds2, turbines):
    levels = own.shape[2]
    last = levels - 1
    sign = place[0].astype(jnp.float32)
    base = place[1]
    step = place[0]

    def at(j):
        return base + step * j

    for field in range(6):
        d, i = divmod(field, 3)
        tangents[field, :, 10:14, :] = own[d, i]
    for c in range(4):
        winds[c, :, 10:14, :] = edge[c].astype(jnp.float32)
        winds2[c, :, 10:14, :] = (edge[4 + c] if c < 3 else visc[0]).astype(jnp.float32)
    turbines[:, 10:14, :] = edge[7].astype(jnp.float32)

    def sides(near, far, inner, low_edge, high_edge):
        for field in range(6):
            d, i = divmod(field, 3)
            tangents[field, :, near : near + 4, :] = mate[d, i]
            tangents[field, :, far : far + 4, :] = other[field].astype(jnp.float32)
            first = half * (field % 2)
            low = other[6 + field // 2, first : first + half].astype(jnp.float32)
            tangents[field, :half, inner : inner + 2, :] += low[:, 0:2]
            tangents[field, half:, inner : inner + 2, :] += low[:, 2:4]
        for c in range(4):
            winds[c, :, 6:10, :] = low_edge[c].astype(jnp.float32)
            winds[c, :, 14:18, :] = high_edge[c].astype(jnp.float32)
        turbines[:, 6:10, :] = low_edge[7].astype(jnp.float32)
        turbines[:, 14:18, :] = high_edge[7].astype(jnp.float32)

    half = levels // 2
    pl.when(place[4] == 0)(lambda: sides(14, 6, 8, edge_other, edge_mate))
    pl.when(place[4] == 1)(lambda: sides(6, 14, 14, edge_mate, edge_other))

    def level_rows(j, above, below):
        k = at(j)
        terms = wind_terms(winds, turbines, weights, k, above, below, sign)
        rows = right_side(tangents, terms, k, above, below)
        for c in range(2):
            power_out[c, k] = terms["turbine"] * terms["speed"] * terms["wind"][c]
        wind2 = [window(winds2, c, k) for c in range(2)]
        square = wind2[0] * wind2[0] + wind2[1] * wind2[1]
        scale = terms["turbine"] * (square * lax.rsqrt(square))
        return rows, [scale * wind2[0], scale * wind2[1]]

    def eliminate(j, above, below, carry):
        face_prev, ratio_prev, values_prev, face2_prev, ratio2_prev, w_prev = carry
        k = at(j)
        rows, wrows = level_rows(j, above, below)
        face = FACE * (window(winds, 3, k) + window(winds, 3, above))
        inverse = 1.0 / (1.0 + face + face_prev * (1.0 - ratio_prev))
        ratio = face * inverse
        values = [(r + face_prev * v) * inverse for r, v in zip(rows, values_prev)]
        ratio_out[k] = ratio
        for field in range(6):
            value_out[field, k] = values[field]
        face2 = FACE * (window(winds2, 3, k) + window(winds2, 3, above))
        inverse2 = 1.0 / (1.0 + face2 + face2_prev * (1.0 - ratio2_prev))
        ratio2 = face2 * inverse2
        ws = [(r + face2_prev * v) * inverse2 for r, v in zip(wrows, w_prev)]
        ratio2_out[k] = ratio2
        inverse2_out[k] = inverse2
        face2_out[k] = face2
        for c in range(2):
            wrow_out[c, k] = ws[c]
        return face, ratio, tuple(values), face2, ratio2, tuple(ws)

    zero = jnp.zeros((8, own.shape[4]), jnp.float32)
    carry = (
        (2.0 * FACE) * window(winds, 3, at(0)), zero, (zero,) * 6,
        (2.0 * FACE) * window(winds2, 3, at(0)), zero, (zero,) * 2,
    )
    carry = eliminate(0, at(1), None, carry)
    carry = lax.fori_loop(
        1, last, lambda j, c: eliminate(j, at(j + 1), at(j - 1), c), carry, unroll=UNROLL
    )
    face, ratio, values, face2, ratio2, ws = carry
    k = at(last)
    rows, wrows = level_rows(last, None, at(last - 1))
    for field in range(6):
        message[RHS + field] = rows[field] + face * values[field]
        message[RAW + field] = window(tangents, field, k)
    message[DIAG] = 1.0 + face * (1.0 - ratio)
    message[VISC] = window(winds, 3, k)
    message[DIAG2] = 1.0 + face2 * (1.0 - ratio2)
    message[VISC2] = window(winds2, 3, k)
    for c in range(3):
        message[WIND + c] = window(winds, c, k)
        message[WIND2 + c] = window(winds2, c, k)
    for c in range(2):
        message[WROW + c] = wrows[c] + face2 * ws[c]


SINGLE = ("center", "x_up", "x_down", "x_far", "y_up", "y_down", "y_far", "z")
TERMS = len(SINGLE) + 3 + 9


def terms_kernel(place, weights, edge_mate, edge, edge_other, visc, out, winds, turbines):
    levels = edge.shape[1]
    last = levels - 1
    sign = place[0].astype(jnp.float32)
    base = place[1]
    step = place[0]
    directions = weights.shape[0]

    def at(j):
        return base + step * j

    for c in range(4):
        winds[c, :, 10:14, :] = (edge[4 + c] if c < 3 else visc[0]).astype(jnp.float32)
    turbines[:, 10:14, :] = edge[7].astype(jnp.float32)

    def sides(low_edge, high_edge):
        for c in range(3):
            winds[c, :, 6:10, :] = low_edge[4 + c].astype(jnp.float32)
            winds[c, :, 14:18, :] = high_edge[4 + c].astype(jnp.float32)

    pl.when(place[4] == 0)(lambda: sides(edge_other, edge_mate))
    pl.when(place[4] == 1)(lambda: sides(edge_mate, edge_other))

    def level_terms(j, above, below):
        k = at(j)
        terms = wind_terms(winds, turbines, weights, k, above, below, sign)
        values = [terms[name] for name in SINGLE] + terms["wind"] + terms["force"]
        for part in terms["by"]:
            values += part
        for n, value in enumerate(values):
            out[n, k] = value

    level_terms(0, at(1), None)

    def body(j, carry):
        level_terms(j, at(j + 1), at(j - 1))
        return carry

    lax.fori_loop(1, last, body, 0, unroll=UNROLL)
    level_terms(last, None, at(last - 1))


def stored_terms(store, level):
    terms = {name: store[n, level] for n, name in enumerate(SINGLE)}
    start = len(SINGLE)
    terms["wind"] = [store[start + i, level] for i in range(3)]
    count = store.shape[0] - TERMS
    terms["force"] = [store[start + 3 + d, level] for d in range(count)]
    start += 3 + count
    terms["by"] = [[store[start + 3 * c + i, level] for i in range(3)] for c in range(3)]
    return terms


def second_kernel(scale, place, mine, theirs, ratio_in, value_in, power_in, ratio2_in, inverse2_in,
                  face2_in, wrow_in, store,
                  row_out, value_out, middle_out, sums_out, tangents, adjoint):
    levels = ratio_in.shape[0]
    last = levels - 1
    sign = place[0].astype(jnp.float32)
    base = place[1]
    step = place[0]

    def at(j):
        return base + step * j

    zero = jnp.zeros(ratio_in.shape[1:], jnp.float32)
    layer = lax.broadcasted_iota(jnp.int32, zero.shape, 0)
    inside = jnp.logical_and(layer >= place[2], layer < place[3])
    center = jnp.logical_and(layer >= 2, layer < 6)

    face = FACE * (mine[VISC] + theirs[VISC])
    pivot, pivot_far = mine[DIAG] + face, theirs[DIAG] + face
    inverse = 1.0 / (pivot * pivot_far - face * face)
    nexts, beyond = [], []
    for field in range(6):
        d, i = divmod(field, 3)
        row = mine[RHS + field] - (HALF * sign) * (
            mine[WIND + 2] * theirs[RAW + field] + mine[RAW + 3 * d + 2] * theirs[WIND + i]
        )
        row_far = theirs[RHS + field] + (HALF * sign) * (
            theirs[WIND + 2] * mine[RAW + field] + theirs[RAW + 3 * d + 2] * mine[WIND + i]
        )
        nexts.append(jnp.where(inside, (row * pivot_far + face * row_far) * inverse, 0.0))
        beyond.append(jnp.where(inside, (row_far * pivot + face * row) * inverse, 0.0))
    face2 = FACE * (mine[VISC2] + theirs[VISC2])
    pivot, pivot_far = mine[DIAG2] + face2, theirs[DIAG2] + face2
    inverse = 1.0 / (pivot * pivot_far - face2 * face2)
    near_part, far_part = pivot_far * inverse, face2 * inverse
    middle_out[0] = near_part
    middle_out[1] = far_part
    ws = [near_part * mine[WROW + c] + far_part * theirs[WROW + c] for c in range(2)]

    def keep(k, values, ws, sums):
        for field in range(6):
            tangents[field, k, 8:16, :] = values[field]
        for c in range(2):
            adjoint[c, k] = ws[c]
        return tuple(
            sums[d] + power_in[0, k] * values[3 * d] + power_in[1, k] * values[3 * d + 1]
            for d in range(2)
        )

    sums = keep(at(last), nexts, ws, (zero, zero))

    def back(n, carry):
        values, ws, sums = carry
        k = at(last - 1 - n)
        ratio = ratio_in[k]
        values = tuple(
            jnp.where(inside, value_in[f, k] + ratio * values[f], 0.0) for f in range(6)
        )
        ratio2 = ratio2_in[k]
        ws = tuple(wrow_in[c, k] + ratio2 * ws[c] for c in range(2))
        return values, ws, keep(k, values, ws, sums)

    _, _, sums = lax.fori_loop(0, last, back, (tuple(nexts), tuple(ws), sums), unroll=True)

    def level_rows(j, above, below, sums, values_beyond=None):
        k = at(j)
        terms = stored_terms(store, k)
        if values_beyond is not None:
            for i in range(3):
                terms["by"][2][i] += (HALF * sign) * theirs[WIND2 + i]
        rows = right_side(tangents, terms, k, above, below, values_beyond)
        sums = tuple(
            sums[d] + adjoint[0, k] * rows[3 * d] + adjoint[1, k] * rows[3 * d + 1]
            for d in range(2)
        )
        return rows, sums

    def eliminate(j, above, below, carry):
        face_prev, values_prev, sums = carry
        k = at(j)
        rows, sums = level_rows(j, above, below, sums)
        inverse = inverse2_in[k]
        values = tuple((r + face_prev * v) * inverse for r, v in zip(rows, values_prev))
        for field in range(6):
            value_out[field, k] = values[field]
        return face2_in[k], values, sums

    carry = eliminate(0, at(1), None, (zero, (zero,) * 6, sums))
    face, values, sums = lax.fori_loop(
        1, last, lambda j, c: eliminate(j, at(j + 1), at(j - 1), c), carry, unroll=UNROLL
    )
    rows, sums = level_rows(last, None, at(last - 1), sums, beyond)
    for field in range(6):
        row_out[field] = rows[field] + face * values[field]
    for d in range(2):
        sums_out[d : d + 1, :] = scale * jnp.sum(
            jnp.where(center, sums[d], 0.0), axis=0, keepdims=True
        )


def third_kernel(place, mine, theirs, middle, ratio_in, value_in, out):
    levels = ratio_in.shape[0]
    last = levels - 1
    base = place[1]
    step = place[0]
    values = tuple(middle[0] * mine[f] + middle[1] * theirs[f] for f in range(6))

    def keep(k, values):
        for field in range(6):
            d, i = divmod(field, 3)
            out[d, i, k] = values[field][2:6]

    keep(base + step * last, values)

    def back(n, values):
        k = base + step * (last - 1 - n)
        ratio = ratio_in[k]
        values = tuple(value_in[f, k] + ratio * values[f] for f in range(6))
        keep(k, values)
        return values

    lax.fori_loop(0, last, back, values, unroll=True)


def call(kernel, scalars, arrays, outs, scratch):
    return pl.pallas_call(
        kernel,
        out_shape=[jax.ShapeDtypeStruct(shape, jnp.float32) for shape in outs],
        in_specs=[pl.BlockSpec(memory_space=pltpu.SMEM)] * len(scalars)
        + [pl.BlockSpec(memory_space=pltpu.VMEM)] * len(arrays),
        out_specs=[pl.BlockSpec(memory_space=pltpu.VMEM)] * len(outs),
        scratch_shapes=[pltpu.VMEM(shape, jnp.float32) for shape in scratch],
        compiler_params=pltpu.CompilerParams(vmem_limit_bytes=40 * 1024 * 1024),
    )(*scalars, *arrays)


def prepare_kernel(slots, steps, records, groups, tangent, code, both, send, mask, packed,
                   groups_here, own, rest, arrived):
    per_device, fields = records.shape[0], records.shape[1]
    owners = slots.shape[0] // per_device
    slot_a, slot_b = slots[steps[0]], slots[steps[1]]
    owner_b = lax.div(slot_b, per_device)
    chosen = jnp.where(lax.axis_index("dir") == owner_b, slot_b, slot_a)
    targets = (send, both.at[0:fields], both.at[fields : 2 * fields])
    copies = [
        pltpu.make_async_copy(records.at[lax.rem(slot, per_device)], target, arrived.at[n])
        for n, (slot, target) in enumerate(zip((chosen, slot_a, slot_b), targets))
    ]
    copies.append(pltpu.make_async_copy(groups, groups_here, arrived.at[3]))
    copies.append(pltpu.make_async_copy(tangent, own, arrived.at[4]))
    for copy in copies:
        copy.start()
    code[0] = lax.div(slot_a, per_device) * owners + owner_b
    copies[3].wait()
    mask[0] = groups_here[...].astype(jnp.float32).astype(mask.dtype)
    copies[4].wait()
    half = rest.shape[0]

    def pack(inner):
        for field in range(6):
            d, i = divmod(field, 3)
            packed[field] = own[d, i].astype(packed.dtype)
            near = own[d, i, :, inner : inner + 2, :]
            near = near - near.astype(packed.dtype).astype(jnp.float32)
            rest[:, 0:2, :] = near[:half]
            rest[:, 2:4, :] = near[half:]
            first = half * (field % 2)
            packed[6 + field // 2, first : first + half] = rest[...].astype(packed.dtype)

    core = lax.axis_index("core")
    pl.when(core == 0)(lambda: pack(0))
    pl.when(core == 1)(lambda: pack(2))
    for copy in copies[:3]:
        copy.wait()


def prepare(record_slot, step_record, records, turbine_mask, tangent_in):
    fields, *block = records.shape[1:]
    shapes = [(2 * fields, *block), (fields, *block), (1, *block), (9, *block)]
    return pl.pallas_call(
        prepare_kernel,
        out_shape=[jax.ShapeDtypeStruct((1,), jnp.int32)]
        + [jax.ShapeDtypeStruct(shape, records.dtype) for shape in shapes],
        in_specs=[pl.BlockSpec(memory_space=pltpu.SMEM)] * 2 + [pl.BlockSpec(memory_space=pl.ANY)] * 3,
        out_specs=[pl.BlockSpec(memory_space=pltpu.SMEM)] + [pl.BlockSpec(memory_space=pltpu.VMEM)] * 4,
        scratch_shapes=[
            pltpu.VMEM(turbine_mask.shape, turbine_mask.dtype),
            pltpu.VMEM(tangent_in.shape, tangent_in.dtype),
            pltpu.VMEM((block[0] // 2, *block[1:]), jnp.float32),
            pltpu.SemaphoreType.DMA((5,)),
        ],
    )(record_slot, step_record, records, turbine_mask, tangent_in)


def from_mate(block):
    return lax.ppermute(block, "core", [(0, 1), (1, 0)])


def from_other(block):
    count = lax.axis_size("row")
    pairs = [(2 * i + 1, 2 * i + 2) for i in range(count - 1)]
    pairs += [(right, left) for left, right in pairs]
    return lax.ppermute(block, TILE, pairs)


def gather_inputs(code, both, send, tangent_in, packed, mask):
    count = lax.axis_size("dir")
    here = lax.axis_index("dir")
    fields = send.shape[0]

    def take(record, owner, got):
        for k, piece in enumerate(got, 1):
            record = jnp.where(here == (owner + k) % count, piece, record)
        return record

    def branch(a, b):
        def run(both, send, tangent, packed, mask):
            block = both if a == b else send
            got = [
                lax.ppermute(block, "dir", [(o, (o + k) % count) for o in sorted({a, b})])
                for k in range(1, count)
            ]
            tangents = from_mate(tangent), from_other(packed)
            if a == b:
                recs = take(both, a, got)
                recs, visc = recs[:-1], recs[-1:]
            else:
                rec_b = take(both[fields:], b, got)
                recs = jnp.concatenate([take(both[:fields], a, got), rec_b[:-1]], axis=0)
                visc = rec_b[-1:]
            edge = jnp.concatenate([recs, mask], axis=0)
            return edge, visc, *tangents, from_mate(edge), from_other(edge)

        return run

    branches = [branch(a, b) for a in range(count) for b in range(count)]
    return lax.switch(code, branches, both, send, tangent_in, packed, mask)


def shards(tangent_in, records, record_slot, step_record, turbine_mask, group_weights):
    directions, components, levels, layers, spans = tangent_in.shape
    fields = directions * components
    tiles = lax.axis_size("row") * lax.axis_size("core")
    tile = lax.axis_index("row") * lax.axis_size("core") + lax.axis_index("core")
    vert = lax.axis_index("vert")
    swap = [(0, 1), (1, 0)]

    place = jnp.stack([
        1 - 2 * vert,
        vert * (levels - 1),
        jnp.where(tile == 0, 2, 0),
        jnp.where(tile == tiles - 1, 6, 8),
        lax.axis_index("core"),
    ]).astype(jnp.int32)

    code, both, send, mask, packed = prepare(
        record_slot, step_record, records, turbine_mask, tangent_in
    )
    edge, visc, mate, other, edge_mate, edge_other = gather_inputs(
        code[0], both, send, tangent_in, packed, mask
    )

    def block(*lead):
        return (*lead, 8, spans)

    def wide(*lead):
        return (*lead, 24, spans)

    message, ratio, value, power, ratio2, inverse2, face2, wrow = call(
        first_kernel,
        (place, group_weights),
        (mate, tangent_in, other, edge_mate, edge, edge_other, visc),
        (block(FIELDS), block(levels), block(fields, levels), block(2, levels),
         block(levels), block(levels), block(levels), block(2, levels)),
        (wide(fields, levels), wide(4, levels), wide(4, levels), wide(levels)),
    )
    answer = lax.ppermute(message, "vert", swap)
    (store,) = call(
        terms_kernel,
        (place, group_weights),
        (edge_mate, edge, edge_other, visc),
        (block(TERMS + directions, levels),),
        (wide(4, levels), wide(levels)),
    )
    cells = levels * lax.axis_size("vert") * layers * tiles * spans
    row, value2, middle, sums = call(
        functools.partial(second_kernel, POWER_SCALE / math.sqrt(cells)),
        (place,),
        (message, answer, ratio, value, power, ratio2, inverse2, face2, wrow, store),
        (block(fields), block(fields, levels), block(2), (directions, spans)),
        (wide(fields, levels), block(2, levels)),
    )
    answer2 = lax.ppermute(row, "vert", swap)

    sums = lax.psum(sums, "core")
    count = lax.axis_size("row") * lax.axis_size("vert")
    gathered = lax.all_to_all(
        jnp.broadcast_to(sums[None], (count, directions, spans)), ("row", "vert"), 0, 0, tiled=True
    )
    power_out = jnp.sum(gathered, axis=(0, 2))

    (tangent_out,) = call(
        third_kernel,
        (place,),
        (row, answer2, middle, ratio2, value2),
        (tangent_in.shape,),
        (),
    )
    return tangent_out, power_out


def solution(mesh):
    tiles, verts, dirs = mesh.devices.shape
    fine = Mesh(mesh.devices.reshape(tiles // 2, 2, verts, dirs), (*TILE, "vert", "dir"))
    in_specs = (
        P("dir", None, "vert", TILE, None),
        P("dir", None, "vert", TILE, None),
        P(),
        P(),
        P("vert", TILE, None),
        P("dir", None),
    )
    out_specs = (P("dir", None, "vert", TILE, None), P("dir"))
    return jax.shard_map(shards, mesh=fine, in_specs=in_specs, out_specs=out_specs, check_vma=False)
```

```python
import functools
import math

import jax
import jax.numpy as jnp
from jax import lax
from jax.experimental import pallas as pl
from jax.experimental.pallas import tpu as pltpu
from jax.sharding import Mesh
from jax.sharding import PartitionSpec as P

STEPS = 2
TIME_STEP = 0.05
DRAG_COEFF = 0.5
POWER_SCALE = 0.01
VERTICAL_ASPECT = 400.0
TILE = ("row", "core")
UNROLL = 15
HALF = 0.5 * TIME_STEP
FACE = 0.5 * TIME_STEP * VERTICAL_ASPECT

RHS, DIAG, VISC, WIND, RAW, DIAG2, VISC2, WIND2, WROW, FIELDS = 0, 6, 7, 8, 11, 17, 18, 19, 22, 24


def window(ref, field, level, offset=0):
    return ref[field, level, 8 + offset : 16 + offset, :]


def roll_y(values, offset):
    return pltpu.roll(values, (-offset) % values.shape[-1], 1)


def wind_terms(winds, turbines, weights, level, above, below, sign):
    wind = [window(winds, c, level) for c in range(3)]
    visc = TIME_STEP * window(winds, 3, level)
    mask = turbines[level, 8:16, :]
    turbine = jnp.where(mask > 0.5, 1.0, 0.0)
    square = wind[0] * wind[0] + wind[1] * wind[1]
    inverse = lax.rsqrt(square)
    speed = square * inverse
    drag = (DRAG_COEFF * TIME_STEP) * turbine
    along = drag * inverse
    by_first, by_second, by_third = [], [], []
    for c in range(3):
        near = window(winds, c, level, 1) - window(winds, c, level, -1)
        far = window(winds, c, level, 2) - window(winds, c, level, -2)
        slope = (TIME_STEP * 8.0 / 12.0) * near - (TIME_STEP / 12.0) * far
        by_first.append(slope + along * wind[c] * wind[0])
        near = roll_y(wind[c], 1) - roll_y(wind[c], -1)
        far = roll_y(wind[c], 2) - roll_y(wind[c], -2)
        slope = (TIME_STEP * 8.0 / 12.0) * near - (TIME_STEP / 12.0) * far
        by_second.append(slope + along * wind[c] * wind[1])
        vertical = jnp.zeros_like(speed)
        if above is not None:
            vertical = vertical + window(winds, c, above)
        if below is not None:
            vertical = vertical - window(winds, c, below)
        by_third.append((HALF * sign) * vertical)
    speed_step = TIME_STEP * speed
    force = []
    for d in range(weights.shape[0]):
        source = jnp.zeros_like(speed_step)
        for g in range(weights.shape[1]):
            source = jnp.where(mask == float(g + 1), weights[d, g], source)
        force.append(source * speed_step)
    first = (TIME_STEP * 8.0 / 12.0) * wind[0]
    second = (TIME_STEP * 8.0 / 12.0) * wind[1]
    return dict(
        wind=wind,
        force=force,
        turbine=turbine,
        speed=speed,
        center=1.0 - 4.0 * visc - drag * speed,
        x_up=visc - first,
        x_down=visc + first,
        x_far=0.125 * first,
        y_up=visc - second,
        y_down=visc + second,
        y_far=0.125 * second,
        z=(HALF * sign) * wind[2],
        by=(by_first, by_second, by_third),
    )


def right_side(tangents, terms, level, above, below, beyond=None):
    rows = []
    for d, force in enumerate(terms["force"]):
        own = [window(tangents, 3 * d + i, level) for i in range(3)]
        for i in range(3):
            field = 3 * d + i
            value = terms["center"] * own[i]
            value += terms["x_up"] * window(tangents, field, level, 1)
            value += terms["x_down"] * window(tangents, field, level, -1)
            value += terms["x_far"] * (
                window(tangents, field, level, 2) - window(tangents, field, level, -2)
            )
            value += terms["y_up"] * roll_y(own[i], 1)
            value += terms["y_down"] * roll_y(own[i], -1)
            value += terms["y_far"] * (roll_y(own[i], 2) - roll_y(own[i], -2))
            vertical = None
            if beyond is not None:
                vertical = beyond[field]
            elif above is not None:
                vertical = window(tangents, field, above)
            if below is not None:
                lower = window(tangents, field, below)
                vertical = -lower if vertical is None else vertical - lower
            if vertical is not None:
                value -= terms["z"] * vertical
            for c in range(3):
                value -= terms["by"][c][i] * own[c]
            value -= force * terms["wind"][i]
            rows.append(value)
    return rows


def first_kernel(place, weights, mate, own, other, edge_mate, edge, edge_other, visc,
                 message, ratio_out, value_out, power_out, ratio2_out, inverse2_out, face2_out,
                 wrow_out, tangents, winds, winds2, turbines):
    levels = own.shape[2]
    last = levels - 1
    sign = place[0].astype(jnp.float32)
    base = place[1]
    step = place[0]

    def at(j):
        return base + step * j

    for field in range(6):
        d, i = divmod(field, 3)
        tangents[field, :, 10:14, :] = own[d, i]
    for c in range(4):
        winds[c, :, 10:14, :] = edge[c].astype(jnp.float32)
        winds2[c, :, 10:14, :] = (edge[4 + c] if c < 3 else visc[0]).astype(jnp.float32)
    turbines[:, 10:14, :] = edge[7].astype(jnp.float32)

    def sides(near, far, inner, low_edge, high_edge):
        for field in range(6):
            d, i = divmod(field, 3)
            tangents[field, :, near : near + 4, :] = mate[d, i]
            tangents[field, :, far : far + 4, :] = other[field].astype(jnp.float32)
            first = half * (field % 2)
            low = other[6 + field // 2, first : first + half].astype(jnp.float32)
            tangents[field, :half, inner : inner + 2, :] += low[:, 0:2]
            tangents[field, half:, inner : inner + 2, :] += low[:, 2:4]
        for c in range(4):
            winds[c, :, 6:10, :] = low_edge[c].astype(jnp.float32)
            winds[c, :, 14:18, :] = high_edge[c].astype(jnp.float32)
        turbines[:, 6:10, :] = low_edge[7].astype(jnp.float32)
        turbines[:, 14:18, :] = high_edge[7].astype(jnp.float32)

    half = levels // 2
    pl.when(place[4] == 0)(lambda: sides(14, 6, 8, edge_other, edge_mate))
    pl.when(place[4] == 1)(lambda: sides(6, 14, 14, edge_mate, edge_other))

    def level_rows(j, above, below):
        k = at(j)
        terms = wind_terms(winds, turbines, weights, k, above, below, sign)
        rows = right_side(tangents, terms, k, above, below)
        for c in range(2):
            power_out[c, k] = terms["turbine"] * terms["speed"] * terms["wind"][c]
        wind2 = [window(winds2, c, k) for c in range(2)]
        square = wind2[0] * wind2[0] + wind2[1] * wind2[1]
        scale = terms["turbine"] * (square * lax.rsqrt(square))
        return rows, [scale * wind2[0], scale * wind2[1]]

    def eliminate(j, above, below, carry):
        face_prev, ratio_prev, values_prev, face2_prev, ratio2_prev, w_prev = carry
        k = at(j)
        rows, wrows = level_rows(j, above, below)
        face = FACE * (window(winds, 3, k) + window(winds, 3, above))
        inverse = 1.0 / (1.0 + face + face_prev * (1.0 - ratio_prev))
        ratio = face * inverse
        values = [(r + face_prev * v) * inverse for r, v in zip(rows, values_prev)]
        ratio_out[k] = ratio
        for field in range(6):
            value_out[field, k] = values[field]
        face2 = FACE * (window(winds2, 3, k) + window(winds2, 3, above))
        inverse2 = 1.0 / (1.0 + face2 + face2_prev * (1.0 - ratio2_prev))
        ratio2 = face2 * inverse2
        ws = [(r + face2_prev * v) * inverse2 for r, v in zip(wrows, w_prev)]
        ratio2_out[k] = ratio2
        inverse2_out[k] = inverse2
        face2_out[k] = face2
        for c in range(2):
            wrow_out[c, k] = ws[c]
        return face, ratio, tuple(values), face2, ratio2, tuple(ws)

    zero = jnp.zeros((8, own.shape[4]), jnp.float32)
    carry = (
        (2.0 * FACE) * window(winds, 3, at(0)), zero, (zero,) * 6,
        (2.0 * FACE) * window(winds2, 3, at(0)), zero, (zero,) * 2,
    )
    carry = eliminate(0, at(1), None, carry)
    carry = lax.fori_loop(
        1, last, lambda j, c: eliminate(j, at(j + 1), at(j - 1), c), carry, unroll=UNROLL
    )
    face, ratio, values, face2, ratio2, ws = carry
    k = at(last)
    rows, wrows = level_rows(last, None, at(last - 1))
    for field in range(6):
        message[RHS + field] = rows[field] + face * values[field]
        message[RAW + field] = window(tangents, field, k)
    message[DIAG] = 1.0 + face * (1.0 - ratio)
    message[VISC] = window(winds, 3, k)
    message[DIAG2] = 1.0 + face2 * (1.0 - ratio2)
    message[VISC2] = window(winds2, 3, k)
    for c in range(3):
        message[WIND + c] = window(winds, c, k)
        message[WIND2 + c] = window(winds2, c, k)
    for c in range(2):
        message[WROW + c] = wrows[c] + face2 * ws[c]


SINGLE = ("center", "x_up", "x_down", "x_far", "y_up", "y_down", "y_far", "z")
TERMS = len(SINGLE) + 3 + 9


def terms_kernel(place, weights, edge_mate, edge, edge_other, visc, out, winds, turbines):
    levels = edge.shape[1]
    last = levels - 1
    sign = place[0].astype(jnp.float32)
    base = place[1]
    step = place[0]
    directions = weights.shape[0]

    def at(j):
        return base + step * j

    for c in range(4):
        winds[c, :, 10:14, :] = (edge[4 + c] if c < 3 else visc[0]).astype(jnp.float32)
    turbines[:, 10:14, :] = edge[7].astype(jnp.float32)

    def sides(low_edge, high_edge):
        for c in range(3):
            winds[c, :, 6:10, :] = low_edge[4 + c].astype(jnp.float32)
            winds[c, :, 14:18, :] = high_edge[4 + c].astype(jnp.float32)

    pl.when(place[4] == 0)(lambda: sides(edge_other, edge_mate))
    pl.when(place[4] == 1)(lambda: sides(edge_mate, edge_other))

    def level_terms(j, above, below):
        k = at(j)
        terms = wind_terms(winds, turbines, weights, k, above, below, sign)
        values = [terms[name] for name in SINGLE] + terms["wind"] + terms["force"]
        for part in terms["by"]:
            values += part
        for n, value in enumerate(values):
            out[n, k] = value

    level_terms(0, at(1), None)

    def body(j, carry):
        level_terms(j, at(j + 1), at(j - 1))
        return carry

    lax.fori_loop(1, last, body, 0, unroll=UNROLL)
    level_terms(last, None, at(last - 1))


def stored_terms(store, level):
    terms = {name: store[n, level] for n, name in enumerate(SINGLE)}
    start = len(SINGLE)
    terms["wind"] = [store[start + i, level] for i in range(3)]
    count = store.shape[0] - TERMS
    terms["force"] = [store[start + 3 + d, level] for d in range(count)]
    start += 3 + count
    terms["by"] = [[store[start + 3 * c + i, level] for i in range(3)] for c in range(3)]
    return terms


def second_kernel(scale, place, mine, theirs, ratio_in, value_in, power_in, ratio2_in, inverse2_in,
                  face2_in, wrow_in, store,
                  row_out, value_out, middle_out, sums_out, tangents, adjoint):
    levels = ratio_in.shape[0]
    last = levels - 1
    sign = place[0].astype(jnp.float32)
    base = place[1]
    step = place[0]

    def at(j):
        return base + step * j

    zero = jnp.zeros(ratio_in.shape[1:], jnp.float32)
    layer = lax.broadcasted_iota(jnp.int32, zero.shape, 0)
    inside = jnp.logical_and(layer >= place[2], layer < place[3])
    center = jnp.logical_and(layer >= 2, layer < 6)

    face = FACE * (mine[VISC] + theirs[VISC])
    pivot, pivot_far = mine[DIAG] + face, theirs[DIAG] + face
    inverse = 1.0 / (pivot * pivot_far - face * face)
    nexts, beyond = [], []
    for field in range(6):
        d, i = divmod(field, 3)
        row = mine[RHS + field] - (HALF * sign) * (
            mine[WIND + 2] * theirs[RAW + field] + mine[RAW + 3 * d + 2] * theirs[WIND + i]
        )
        row_far = theirs[RHS + field] + (HALF * sign) * (
            theirs[WIND + 2] * mine[RAW + field] + theirs[RAW + 3 * d + 2] * mine[WIND + i]
        )
        nexts.append(jnp.where(inside, (row * pivot_far + face * row_far) * inverse, 0.0))
        beyond.append(jnp.where(inside, (row_far * pivot + face * row) * inverse, 0.0))
    face2 = FACE * (mine[VISC2] + theirs[VISC2])
    pivot, pivot_far = mine[DIAG2] + face2, theirs[DIAG2] + face2
    inverse = 1.0 / (pivot * pivot_far - face2 * face2)
    near_part, far_part = pivot_far * inverse, face2 * inverse
    middle_out[0] = near_part
    middle_out[1] = far_part
    ws = [near_part * mine[WROW + c] + far_part * theirs[WROW + c] for c in range(2)]

    def keep(k, values, ws, sums):
        for field in range(6):
            tangents[field, k, 8:16, :] = values[field]
        for c in range(2):
            adjoint[c, k] = ws[c]
        return tuple(
            sums[d] + power_in[0, k] * values[3 * d] + power_in[1, k] * values[3 * d + 1]
            for d in range(2)
        )

    sums = keep(at(last), nexts, ws, (zero, zero))

    def back(n, carry):
        values, ws, sums = carry
        k = at(last - 1 - n)
        ratio = ratio_in[k]
        values = tuple(
            jnp.where(inside, value_in[f, k] + ratio * values[f], 0.0) for f in range(6)
        )
        ratio2 = ratio2_in[k]
        ws = tuple(wrow_in[c, k] + ratio2 * ws[c] for c in range(2))
        return values, ws, keep(k, values, ws, sums)

    _, _, sums = lax.fori_loop(0, last, back, (tuple(nexts), tuple(ws), sums), unroll=True)

    def level_rows(j, above, below, sums, values_beyond=None):
        k = at(j)
        terms = stored_terms(store, k)
        if values_beyond is not None:
            for i in range(3):
                terms["by"][2][i] += (HALF * sign) * theirs[WIND2 + i]
        rows = right_side(tangents, terms, k, above, below, values_beyond)
        sums = tuple(
            sums[d] + adjoint[0, k] * rows[3 * d] + adjoint[1, k] * rows[3 * d + 1]
            for d in range(2)
        )
        return rows, sums

    def eliminate(j, above, below, carry):
        face_prev, values_prev, sums = carry
        k = at(j)
        rows, sums = level_rows(j, above, below, sums)
        inverse = inverse2_in[k]
        values = tuple((r + face_prev * v) * inverse for r, v in zip(rows, values_prev))
        for field in range(6):
            value_out[field, k] = values[field]
        return face2_in[k], values, sums

    carry = eliminate(0, at(1), None, (zero, (zero,) * 6, sums))
    face, values, sums = lax.fori_loop(
        1, last, lambda j, c: eliminate(j, at(j + 1), at(j - 1), c), carry, unroll=UNROLL
    )
    rows, sums = level_rows(last, None, at(last - 1), sums, beyond)
    for field in range(6):
        row_out[field] = rows[field] + face * values[field]
    for d in range(2):
        sums_out[d : d + 1, :] = scale * jnp.sum(
            jnp.where(center, sums[d], 0.0), axis=0, keepdims=True
        )


def third_kernel(place, mine, theirs, middle, ratio_in, value_in, out):
    levels = ratio_in.shape[0]
    last = levels - 1
    base = place[1]
    step = place[0]
    values = tuple(middle[0] * mine[f] + middle[1] * theirs[f] for f in range(6))

    def keep(k, values):
        for field in range(6):
            d, i = divmod(field, 3)
            out[d, i, k] = values[field][2:6]

    keep(base + step * last, values)

    def back(n, values):
        k = base + step * (last - 1 - n)
        ratio = ratio_in[k]
        values = tuple(value_in[f, k] + ratio * values[f] for f in range(6))
        keep(k, values)
        return values

    lax.fori_loop(0, last, back, values, unroll=True)


def call(kernel, scalars, arrays, outs, scratch):
    return pl.pallas_call(
        kernel,
        out_shape=[jax.ShapeDtypeStruct(shape, jnp.float32) for shape in outs],
        in_specs=[pl.BlockSpec(memory_space=pltpu.SMEM)] * len(scalars)
        + [pl.BlockSpec(memory_space=pltpu.VMEM)] * len(arrays),
        out_specs=[pl.BlockSpec(memory_space=pltpu.VMEM)] * len(outs),
        scratch_shapes=[pltpu.VMEM(shape, jnp.float32) for shape in scratch],
        compiler_params=pltpu.CompilerParams(vmem_limit_bytes=40 * 1024 * 1024),
    )(*scalars, *arrays)


def prepare_kernel(slots, steps, records, groups, tangent, code, both, send, mask, packed,
                   groups_here, own, rest, arrived):
    per_device, fields = records.shape[0], records.shape[1]
    owners = slots.shape[0] // per_device
    slot_a, slot_b = slots[steps[0]], slots[steps[1]]
    owner_b = lax.div(slot_b, per_device)
    chosen = jnp.where(lax.axis_index("dir") == owner_b, slot_b, slot_a)
    targets = (send, both.at[0:fields], both.at[fields : 2 * fields])
    copies = [
        pltpu.make_async_copy(records.at[lax.rem(slot, per_device)], target, arrived.at[n])
        for n, (slot, target) in enumerate(zip((chosen, slot_a, slot_b), targets))
    ]
    copies.append(pltpu.make_async_copy(groups, groups_here, arrived.at[3]))
    copies.append(pltpu.make_async_copy(tangent, own, arrived.at[4]))
    for copy in copies:
        copy.start()
    code[0] = lax.div(slot_a, per_device) * owners + owner_b
    copies[3].wait()
    mask[0] = groups_here[...].astype(jnp.float32).astype(mask.dtype)
    copies[4].wait()
    half = rest.shape[0]

    def pack(inner):
        for field in range(6):
            d, i = divmod(field, 3)
            packed[field] = own[d, i].astype(packed.dtype)
            near = own[d, i, :, inner : inner + 2, :]
            near = near - near.astype(packed.dtype).astype(jnp.float32)
            rest[:, 0:2, :] = near[:half]
            rest[:, 2:4, :] = near[half:]
            first = half * (field % 2)
            packed[6 + field // 2, first : first + half] = rest[...].astype(packed.dtype)

    core = lax.axis_index("core")
    pl.when(core == 0)(lambda: pack(0))
    pl.when(core == 1)(lambda: pack(2))
    for copy in copies[:3]:
        copy.wait()


def prepare(record_slot, step_record, records, turbine_mask, tangent_in):
    fields, *block = records.shape[1:]
    shapes = [(2 * fields, *block), (fields, *block), (1, *block), (9, *block)]
    return pl.pallas_call(
        prepare_kernel,
        out_shape=[jax.ShapeDtypeStruct((1,), jnp.int32)]
        + [jax.ShapeDtypeStruct(shape, records.dtype) for shape in shapes],
        in_specs=[pl.BlockSpec(memory_space=pltpu.SMEM)] * 2 + [pl.BlockSpec(memory_space=pl.ANY)] * 3,
        out_specs=[pl.BlockSpec(memory_space=pltpu.SMEM)] + [pl.BlockSpec(memory_space=pltpu.VMEM)] * 4,
        scratch_shapes=[
            pltpu.VMEM(turbine_mask.shape, turbine_mask.dtype),
            pltpu.VMEM(tangent_in.shape, tangent_in.dtype),
            pltpu.VMEM((block[0] // 2, *block[1:]), jnp.float32),
            pltpu.SemaphoreType.DMA((5,)),
        ],
    )(record_slot, step_record, records, turbine_mask, tangent_in)


def from_mate(block):
    return lax.ppermute(block, "core", [(0, 1), (1, 0)])


def from_other(block):
    count = lax.axis_size("row")
    pairs = [(2 * i + 1, 2 * i + 2) for i in range(count - 1)]
    pairs += [(right, left) for left, right in pairs]
    return lax.ppermute(block, TILE, pairs)


def gather_inputs(code, both, send, tangent_in, packed, mask):
    count = lax.axis_size("dir")
    here = lax.axis_index("dir")
    fields = send.shape[0]

    def take(record, owner, got):
        for k, piece in enumerate(got, 1):
            record = jnp.where(here == (owner + k) % count, piece, record)
        return record

    def branch(a, b):
        def run(both, send, tangent, packed, mask):
            block = both if a == b else send
            got = [
                lax.ppermute(block, "dir", [(o, (o + k) % count) for o in sorted({a, b})])
                for k in range(1, count)
            ]
            tangents = from_mate(tangent), from_other(packed)
            if a == b:
                recs = take(both, a, got)
                recs, visc = recs[:-1], recs[-1:]
            else:
                rec_b = take(both[fields:], b, got)
                recs = jnp.concatenate([take(both[:fields], a, got), rec_b[:-1]], axis=0)
                visc = rec_b[-1:]
            edge = jnp.concatenate([recs, mask], axis=0)
            return edge, visc, *tangents, from_mate(edge), from_other(edge)

        return run

    branches = [branch(a, b) for a in range(count) for b in range(count)]
    return lax.switch(code, branches, both, send, tangent_in, packed, mask)


def shards(tangent_in, records, record_slot, step_record, turbine_mask, group_weights):
    directions, components, levels, layers, spans = tangent_in.shape
    fields = directions * components
    tiles = lax.axis_size("row") * lax.axis_size("core")
    tile = lax.axis_index("row") * lax.axis_size("core") + lax.axis_index("core")
    vert = lax.axis_index("vert")
    swap = [(0, 1), (1, 0)]

    place = jnp.stack([
        1 - 2 * vert,
        vert * (levels - 1),
        jnp.where(tile == 0, 2, 0),
        jnp.where(tile == tiles - 1, 6, 8),
        lax.axis_index("core"),
    ]).astype(jnp.int32)

    code, both, send, mask, packed = prepare(
        record_slot, step_record, records, turbine_mask, tangent_in
    )
    edge, visc, mate, other, edge_mate, edge_other = gather_inputs(
        code[0], both, send, tangent_in, packed, mask
    )

    def block(*lead):
        return (*lead, 8, spans)

    def wide(*lead):
        return (*lead, 24, spans)

    message, ratio, value, power, ratio2, inverse2, face2, wrow = call(
        first_kernel,
        (place, group_weights),
        (mate, tangent_in, other, edge_mate, edge, edge_other, visc),
        (block(FIELDS), block(levels), block(fields, levels), block(2, levels),
         block(levels), block(levels), block(levels), block(2, levels)),
        (wide(fields, levels), wide(4, levels), wide(4, levels), wide(levels)),
    )
    answer = lax.ppermute(message, "vert", swap)
    (store,) = call(
        terms_kernel,
        (place, group_weights),
        (edge_mate, edge, edge_other, visc),
        (block(TERMS + directions, levels),),
        (wide(4, levels), wide(levels)),
    )
    cells = levels * lax.axis_size("vert") * layers * tiles * spans
    row, value2, middle, sums = call(
        functools.partial(second_kernel, POWER_SCALE / math.sqrt(cells)),
        (place,),
        (message, answer, ratio, value, power, ratio2, inverse2, face2, wrow, store),
        (block(fields), block(fields, levels), block(2), (directions, spans)),
        (wide(fields, levels), block(2, levels)),
    )
    answer2 = lax.ppermute(row, "vert", swap)

    sums = lax.psum(sums, "core")
    count = lax.axis_size("row") * lax.axis_size("vert")
    gathered = lax.all_to_all(
        jnp.broadcast_to(sums[None], (count, directions, spans)), ("row", "vert"), 0, 0, tiled=True
    )
    power_out = jnp.sum(gathered, axis=(0, 2))

    (tangent_out,) = call(
        third_kernel,
        (place,),
        (row, answer2, middle, ratio2, value2),
        (tangent_in.shape,),
        (),
    )
    return tangent_out, power_out


def solution(mesh):
    tiles, verts, dirs = mesh.devices.shape
    fine = Mesh(mesh.devices.reshape(tiles // 2, 2, verts, dirs), (*TILE, "vert", "dir"))
    in_specs = (
        P("dir", None, "vert", TILE, None),
        P("dir", None, "vert", TILE, None),
        P(),
        P(),
        P("vert", TILE, None),
        P("dir", None),
    )
    out_specs = (P("dir", None, "vert", TILE, None), P("dir"))
    return jax.shard_map(shards, mesh=fine, in_specs=in_specs, out_specs=out_specs, check_vma=False)
```
